32 devices in a mesh: dp: 4 (over z), expert: 8 (over y, x, core).
Axes of the slice: x: 2, y: 2, z: 4, core: 2. Of those that a mesh axis runs over, the one named last changes fastest.
Arguments:
- tokens_x: bfloat16 [1024, 4096], P('dp', 'expert'), may hold values from -6 to 6
- in_proj: bfloat16 [4096, 1024], P('expert'), may hold values from -0.09375 to 0.09375
- up_weight: bfloat16 [16, 1024, 768], P('expert'), may hold values from -0.1875 to 0.1875
- down_weight: bfloat16 [16, 768, 1024], P('expert'), may hold values from -0.21875 to 0.21875
- expert_ids: int32 [1024, 8], P(('dp', 'expert')), may hold values from 0 to 15, all different within a row; in each aligned block of 32 rows (0 to 31, 32 to 63, ...) at most 24 rows name the same one
- route_probs: float32 [1024, 8], P(('dp', 'expert')), may hold values from 0.05 to 1
- out_grad: bfloat16 [1024, 1024], P(('dp', 'expert')), may hold values from -6 to 6
Outputs:
- combined: bfloat16 [1024, 1024], P(('dp', 'expert'))
- input_grad: bfloat16 [1024, 4096], P('dp', 'expert')
- proj_grad: float32 [4096, 1024], P('expert')
The draws below stay inside these ranges and needn't reach their ends.
Inputs may be any that keep to these rules, and one draw needn't show every extreme that they name: `expert_ids`: each row names 8 different experts. Within the rows of one device (aligned blocks of 32 rows) no expert is named more than 24 times, a bound that some block reaches.
All inputs are finite; a program needn't handle non-finite values.
Results may differ from the reference program's by a relative error of at most 0.019.
Values may be sent and summed in bfloat16 or wider, within the bound.
No kernel may reach another device: no remote copies, remote signals or barrier semaphores. Data moves between devices by JAX's collectives and lax.ppermute only.
A program may use at most 64 MiB of HBM per device.

```python
import math
import jax
import jax.numpy as jnp
import numpy as np
from jax import lax

D = 4096
L = 1024
H = 768
TOP = 8
TOK_DEV = 32
EXPERTS = 16
CAP = 24
TOKENS = 1024
N_DP = 4
N_EXPERT = 8


def with_spikes(array, rng, source, target, parts, factor):
    def block_of(dim):
        return (jnp.arange(array.shape[dim]) // (array.shape[dim] // parts)).reshape((-1,) + (1,) * (array.ndim - 1 - dim))

    near = jax.random.permutation(rng, parts)[block_of(target)]
    other_side = (block_of(target) + parts // 2) % parts
    return jnp.where((block_of(source) == near) | (block_of(source) == other_side), factor * array, array)


def level_of(key, dims, shards, smallest, top_value):
    def one(position, parts):
        draws = jax.random.uniform(jax.random.fold_in(jax.random.fold_in(key, 6), position), (parts,), jnp.float32, smallest / len(shards), top_value / len(shards))
        return jnp.repeat(jnp.exp(draws), dims[position] // parts).reshape((-1,) + (1,) * (len(dims) - position - 1))

    level = one(*shards[0])
    for cut in shards[1:]:
        level = level * one(*cut)
    return level


def shared_out(stream_key, own, number, rows, number_of, top, bound, lean):
    order = jax.random.permutation(stream_key, number_of)
    packed, ordinary = shares(number_of, rows * top, bound, lean, True), shares(number_of, rows * top, bound, lean, False)
    places = jnp.arange(number_of)

    def named(tallies, rotation):
        used = int((tallies > 0).sum())
        fixed = max(1, used // 4)
        moved = fixed + (places - fixed + rotation * (used - fixed)) % max(1, number_of - fixed)
        return jnp.zeros((number_of,), jnp.int32).at[order[jnp.where(places < fixed, places, moved)]].set(jnp.asarray(tallies, jnp.int32))

    tallies = jnp.where(number % 4 == 0, named(packed, number // 4), named(ordinary, number - number // 4 - 1))
    mixed = jax.random.permutation(jax.random.fold_in(own, 3), number_of)
    donor, receiver = mixed[0:number_of // 2 * 2:2], mixed[1:number_of // 2 * 2:2]
    room = jnp.minimum(tallies[donor] - 1, bound - tallies[receiver]) // 2
    room = jnp.where((donor == order[0]) | (receiver == order[0]) | (tallies[receiver] == 0), 0, jnp.maximum(room, 0))
    moved = jax.random.randint(jax.random.fold_in(own, 4), (number_of // 2,), 0, 1 << 20) % (room + 1)
    tallies = tallies.at[donor].add(-moved).at[receiver].add(moved)
    members = jnp.searchsorted(jnp.cumsum(tallies), jnp.arange(rows * top), side="right").astype(jnp.int32)
    listing = members.reshape(top, rows).T
    listing = listing[jax.random.permutation(jax.random.fold_in(own, 1), rows)]
    rotation = jax.random.randint(jax.random.fold_in(own, 2), (rows, 1), 0, top)
    return jnp.take_along_axis(listing, (jnp.arange(top)[None, :] + rotation) % top, axis=1)


def shares(count, total, reach, skew, full):
    weights = [(1 << 20) // math.isqrt(rank ** skew) + 1 for rank in range(1, count + 1)]
    largest = reach if full else min(reach, max(-(-total // count), total * weights[0] // sum(weights)))
    least = 1 if total - largest >= count - 1 else 0
    holding, surplus = [largest] + [least] * (count - 1), total - largest - least * (count - 1)
    while surplus > 0:
        free = [i for i in range(1, count) if holding[i] < largest] or [i for i in range(1, count) if holding[i] < reach]
        pool, remaining = sum([weights[i] for i in free]), surplus
        for i in free:
            addition = min(reach - holding[i], max(1, remaining * weights[i] // pool), surplus)
            holding[i] = holding[i] + addition
            surplus = surplus - addition
    return np.array(holding)


def bell_draw(own_key, extent, deviation, bound, shards=(), held_as=jnp.bfloat16):
    gain = level_of(own_key, extent, shards, -0.22, 0.18) if shards else 1.0
    array = jax.random.normal(own_key, extent, jnp.float32) * deviation * gain
    return jnp.minimum(jnp.maximum(array, -bound), bound).astype(held_as)


def bell_draw_with(own_key, dims, spread, reach, split, heavy, kind=jnp.bfloat16):
    result = spread * jax.random.normal(own_key, dims, jnp.float32)
    if split:
        result = result * level_of(own_key, dims, split, -0.22, 0.18)
    return jnp.clip(with_spikes(result, jax.random.fold_in(own_key, 3), *heavy), -reach, reach).astype(kind)


def setup_inputs(seed: int = 0) -> dict:
    streams_of = jax.random.split(jax.random.key(seed), 8)
    tokens_x = bell_draw_with(streams_of[0], (TOKENS, D), 1.0, 6.0, ((0, 4), (1, 8)), (1, 0, 8, 2.0))
    in_proj = bell_draw(streams_of[1], (D, L), D ** -0.5, 0.09375, ((0, 8),))
    up_weight = bell_draw(streams_of[2], (EXPERTS, L, H), L ** -0.5, 0.1875, ((0, 8),))
    down_weight = bell_draw(streams_of[3], (EXPERTS, H, L), H ** -0.5, 0.21875, ((0, 8),))
    expert_ids_keys = jax.random.split(jax.random.fold_in(streams_of[4], 1), TOKENS // TOK_DEV)
    expert_ids_turns = jax.random.permutation(jax.random.fold_in(streams_of[4], 3), TOKENS // TOK_DEV)
    expert_ids = jax.vmap(lambda own, number: shared_out(jax.random.fold_in(streams_of[4], 2), own, number, TOK_DEV, EXPERTS, TOP, CAP, 2))(expert_ids_keys, expert_ids_turns).reshape((TOKENS, TOP))
    route_probs = jnp.clip(0.05 + 0.95 * jax.random.uniform(streams_of[5], (TOKENS, TOP), jnp.float32) ** level_of(streams_of[5], (TOKENS, TOP), ((0, 32),), -0.2, 0.2), 0.05, 1.0)
    out_grad = bell_draw(streams_of[6], (TOKENS, L), 1.0, 6.0, ((0, 32),))
    return dict(tokens_x=tokens_x, in_proj=in_proj, up_weight=up_weight, down_weight=down_weight, expert_ids=expert_ids, route_probs=route_probs, out_grad=out_grad)


def reference(tokens_x, in_proj, up_weight, down_weight, expert_ids, route_probs, out_grad):
    block_width = D // N_EXPERT

    def add_block(running, block_index):
        first = block_index * block_width
        x_part = lax.dynamic_slice_in_dim(tokens_x, first, block_width, 1)
        w_part = lax.dynamic_slice_in_dim(in_proj, first, block_width, 0)
        term = jnp.dot(x_part, w_part, preferred_element_type=jnp.float32).astype(jnp.bfloat16)
        term = lax.optimization_barrier(term).astype(jnp.float32)
        return running + term, None

    summed, _unused = lax.scan(add_block, jnp.zeros((TOKENS, L), jnp.float32), jnp.arange(N_EXPERT, dtype=jnp.int32))
    latent = summed.astype(jnp.bfloat16)
    flat_ids = expert_ids.reshape(-1)
    flat_probs = route_probs.reshape(-1)
    most_rows = N_DP * N_EXPERT * CAP

    def per_expert(state_pair, expert):
        comb_acc, grad_acc = state_pair
        matches = flat_ids == expert
        count = jnp.sum(matches.astype(jnp.int32))
        chosen = jnp.nonzero(matches, size=most_rows, fill_value=0)[0].astype(jnp.int32)
        in_use = jnp.arange(most_rows, dtype=jnp.int32) < count
        token_index = chosen // TOP
        row_block = latent[token_index]
        prob_pick = jnp.where(in_use, flat_probs[chosen], jnp.float32(0.0))
        grad_rows = (prob_pick[:, None] * out_grad[token_index].astype(jnp.float32)).astype(jnp.bfloat16)
        up_e = up_weight[expert]
        down_e = down_weight[expert]
        preact = jnp.dot(row_block, up_e, preferred_element_type=jnp.float32)
        positive = jnp.maximum(preact, 0.0)
        act_rows = (positive * positive).astype(jnp.bfloat16)
        out_rows = jnp.dot(act_rows, down_e, preferred_element_type=jnp.float32).astype(jnp.bfloat16)
        grad_act = jnp.dot(grad_rows, down_e.T, preferred_element_type=jnp.float32)
        grad_pre = (grad_act * 2.0 * positive).astype(jnp.bfloat16)
        lat_grad = jnp.dot(grad_pre, up_e.T, preferred_element_type=jnp.float32).astype(jnp.bfloat16)
        comb_acc = comb_acc.at[token_index].add(prob_pick[:, None] * out_rows.astype(jnp.float32))
        grad_acc = grad_acc.at[token_index].add(jnp.where(in_use[:, None], lat_grad.astype(jnp.float32), jnp.float32(0.0)))
        return (comb_acc, grad_acc), None

    zeros_rows = jnp.zeros((TOKENS, L), jnp.float32)
    (comb_acc, grad_acc), _unused2 = lax.scan(per_expert, (zeros_rows, zeros_rows), jnp.arange(EXPERTS, dtype=jnp.int32))
    combined = comb_acc.astype(jnp.bfloat16)
    latent_grad = grad_acc.astype(jnp.bfloat16)
    input_grad = jnp.dot(latent_grad, in_proj.T, preferred_element_type=jnp.float32).astype(jnp.bfloat16)
    proj_grad = lax.dot_general(tokens_x, latent_grad, (((0,), (0,)), ((), ())), preferred_element_type=jnp.float32)
    return (combined, input_grad, proj_grad)
```

```python
import jax
import jax.numpy as jnp
from jax import lax
from jax.sharding import PartitionSpec as P


def xor_permute(value, axis, mask):
    size = lax.axis_size(axis)
    return lax.ppermute(value, axis, [(i, i ^ mask) for i in range(size)])


def add_bf16(first, second):
    return (first.astype(jnp.float32) + second.astype(jnp.float32)).astype(jnp.bfloat16)


def dot32(first, second):
    return jnp.dot(first, second, preferred_element_type=jnp.float32)


def dot32_t(first, second):
    return lax.dot_general(
        first, second, (((1,), (1,)), ((), ())), preferred_element_type=jnp.float32
    )


def from_xor_order(pieces, me):
    count = len(pieces)
    rows = pieces[0].shape[0]
    whole = jnp.zeros((count * rows,) + pieces[0].shape[1:], pieces[0].dtype)
    for offset, piece in enumerate(pieces):
        whole = lax.dynamic_update_slice_in_dim(whole, piece, (me ^ offset) * rows, axis=0)
    return whole


def sum_and_gather(summed, gathered, bits):
    for bit in bits:
        sum_rows = summed.shape[0]
        got = xor_permute(jnp.concatenate([summed, gathered], axis=0), "expert", bit)
        summed = add_bf16(summed, got[:sum_rows])
        gathered = jnp.concatenate([gathered, got[sum_rows:]], axis=0)
    return summed, gathered


def order_of(bits):
    masks = [0]
    for bit in bits:
        masks = masks + [mask ^ bit for mask in masks]
    return masks


def scatter_sum(partial, chip, chips):
    rows = partial.shape[0] // chips
    pieces = [
        lax.dynamic_slice_in_dim(partial, (chip ^ k) * rows, rows, axis=0) for k in range(chips)
    ]
    got = [xor_permute(pieces[k], "expert", 2 * k) for k in range(1, chips)]
    total = pieces[0].astype(jnp.float32)
    for piece in got:
        total = total + piece.astype(jnp.float32)
    return total.astype(jnp.bfloat16)


def per_device(tokens_x, in_proj, up_weight, down_weight, expert_ids, route_probs, out_grad):
    owners = lax.axis_size("expert")
    groups = lax.axis_size("dp")
    chips = owners // 2
    me = lax.axis_index("expert")
    core = me % 2
    chip = me // 2
    tok, top = expert_ids.shape
    local_experts = up_weight.shape[0]
    all_experts = local_experts * owners
    features, width = in_proj.shape
    half = chips * tok
    bits = [1 << b for b in range(1, owners.bit_length() - 1)]

    chosen = expert_ids[None, :, :] == jnp.arange(all_experts, dtype=jnp.int32)[:, None, None]
    routing = jnp.sum(jnp.where(chosen, route_probs[None, :, :], 0.0), axis=2).astype(jnp.bfloat16)
    routing = lax.dynamic_update_slice(
        jnp.zeros((all_experts, width), jnp.bfloat16), routing, (0, chip * tok)
    )

    x_cores = tokens_x.reshape(chips, 2, tok, features)
    x_other = lax.dynamic_index_in_dim(x_cores, 1 - core, 1, False).reshape(half, features)
    x_mine = lax.dynamic_index_in_dim(x_cores, core, 1, False).reshape(half, features)
    got = xor_permute(dot32(x_other, in_proj).astype(jnp.bfloat16), "expert", 1)
    summed = add_bf16(dot32(x_mine, in_proj).astype(jnp.bfloat16), got)
    first = jnp.concatenate([summed[: half // 2], routing], axis=0)
    second = summed[half // 2 :]
    first, first_cot = sum_and_gather(first, out_grad[: tok // 2], bits)
    second, second_cot = sum_and_gather(second, out_grad[tok // 2 :], bits[::-1])
    cot = jnp.zeros((chips, 2, tok // 2, width), jnp.bfloat16)
    for position, pieces, order in ((0, first_cot, order_of(bits)), (1, second_cot, order_of(bits[::-1]))):
        pieces = pieces.reshape(chips, 1, 1, tok // 2, width)
        for place, mask in enumerate(order):
            cot = lax.dynamic_update_slice(
                cot, pieces[place], (chip ^ (mask // 2), position, 0, 0)
            )
    mine = jnp.concatenate([first[: half // 2], second, cot.reshape(half, width), first[half // 2 :]], axis=0)
    other = xor_permute(mine, "expert", 1)
    latent = jnp.concatenate([mine[:half], other[:half]], axis=0)
    cot = jnp.concatenate([mine[half : 2 * half], other[half : 2 * half]], axis=0)
    probs = jnp.concatenate([mine[2 * half :, :half], other[2 * half :, :half]], axis=1)
    probs = lax.dynamic_slice_in_dim(probs, me * local_experts, local_experts, axis=0)
    probs = probs.astype(jnp.float32)

    acts, grads = [], []
    for expert in range(local_experts):
        positive = jnp.maximum(dot32(latent, up_weight[expert]), 0.0)
        prob = probs[expert][:, None]
        grad_act = dot32_t(cot, down_weight[expert])
        acts.append((positive * positive * prob).astype(jnp.bfloat16))
        grads.append((grad_act * (2.0 * positive * prob)).astype(jnp.bfloat16))
    lat_part = sum(dot32_t(grads[i], up_weight[i]) for i in range(local_experts)).astype(jnp.bfloat16)
    got = xor_permute(lat_part[half:], "expert", 1)
    latent_grad = scatter_sum(add_bf16(lat_part[:half], got), chip, chips)
    out_part = sum(dot32(acts[i], down_weight[i]) for i in range(local_experts)).astype(jnp.bfloat16)
    got = xor_permute(out_part[half:], "expert", 1)
    combined = scatter_sum(add_bf16(out_part[:half], got), chip, chips)

    gather_groups = groups & (groups - 1) == 0 and groups * owners * tok * width <= 1 << 22
    held = [latent_grad]
    x_held = [tokens_x]
    if gather_groups:
        held += [xor_permute(latent_grad, "dp", m) for m in range(1, groups)]
        x_held += [xor_permute(tokens_x, "dp", m) for m in range(1, groups)]
    count = len(held)
    own = jnp.concatenate(held, axis=0)
    pieces = [own] + [xor_permute(own, "expert", 2 * k) for k in range(1, chips)]
    mine = from_xor_order(pieces, chip).reshape(chips, count, tok, width)
    other = xor_permute(mine, "expert", 1)
    low = jnp.where(core == 0, mine, other)
    high = jnp.where(core == 0, other, mine)
    rows = jnp.stack([low, high], axis=1)
    rows = jnp.transpose(rows, (2, 0, 1, 3, 4)).reshape(count, owners * tok, width)
    input_grad = dot32_t(rows[0], in_proj).astype(jnp.bfloat16)
    proj_grad = lax.dot_general(
        jnp.concatenate(x_held, axis=0),
        rows.reshape(count * owners * tok, width),
        (((0,), (0,)), ((), ())),
        preferred_element_type=jnp.float32,
    )
    if not gather_groups:
        proj_grad = lax.psum(proj_grad, "dp")
    return (combined, input_grad, proj_grad)


def solution(mesh):
    return jax.shard_map(
        per_device,
        mesh=mesh,
        in_specs=(
            P("dp", "expert"),
            P("expert", None),
            P("expert", None, None),
            P("expert", None, None),
            P(("dp", "expert"), None),
            P(("dp", "expert"), None),
            P(("dp", "expert"), None),
        ),
        out_specs=(P(("dp", "expert"), None), P("dp", "expert"), P("expert", None)),
        check_vma=False,
    )
```

```python
import jax
import jax.numpy as jnp
from jax import lax
from jax.experimental import pallas as pl
from jax.experimental.pallas import tpu as pltpu
from jax.sharding import PartitionSpec as P

VMEM = pl.BlockSpec(memory_space=pltpu.VMEM)
ANY = pl.BlockSpec(memory_space=pl.ANY)
BF16 = jnp.bfloat16
F32 = jnp.float32
NN = (((1,), (0,)), ((), ()))
NT = (((1,), (1,)), ((), ()))
TN = (((0,), (0,)), ((), ()))
MIB = 1 << 20


def mxu(first, second, dims=NN):
    return lax.dot_general(first, second, dims, preferred_element_type=F32)


def shape(rows, columns, dtype=BF16):
    return jax.ShapeDtypeStruct((rows, columns), dtype)


def add_bf16(first, second):
    return (first.astype(F32) + second.astype(F32)).astype(BF16)


def local(body, outs, args, name, scratch=(), limit=8, flops=0, ties=()):
    def kernel(*refs):
        body(*refs[: len(args)], *refs[len(args) + len(ties) :])

    single = not isinstance(outs, tuple)
    return pl.pallas_call(
        kernel,
        out_shape=outs,
        in_specs=[VMEM] * len(args) + [ANY] * len(ties),
        out_specs=VMEM if single else tuple(VMEM for _ in outs),
        scratch_shapes=list(scratch),
        compiler_params=pltpu.CompilerParams(vmem_limit_bytes=limit * MIB),
        cost_estimate=pl.CostEstimate(flops=flops, bytes_accessed=MIB, transcendentals=0),
        name=name,
    )(*args, *ties)


def xor_permute(value, axis, mask):
    size = lax.axis_size(axis)
    return lax.ppermute(value, axis, [(i, i ^ mask) for i in range(size)])


def line_gather(value, axis):
    inner, outer = [(1, 2), (2, 1)], [(1, 0), (2, 3)]
    near = xor_permute(value, axis, 1)
    middle = lax.ppermute(value, axis, inner)
    middle_far = lax.ppermute(near, axis, inner)
    edge = lax.ppermute(middle, axis, outer)
    edge_far = lax.ppermute(middle_far, axis, outer)
    return [(near, middle), (middle_far, edge), (edge_far,)]


def hop(hops, index):
    return hops[index] if index < len(hops) else ()


def order_of(bits):
    masks = [0]
    for bit in bits:
        masks = masks + [mask ^ bit for mask in masks]
    return masks


def block(index, rows):
    return pl.ds(pl.multiple_of(index * rows, rows), rows)


def project(x, in_proj, tok):
    rows, features = x.shape
    width = in_proj.shape[1]
    owners = rows // tok
    half = rows // 2

    def body(x_ref, proj_ref, other_ref, mine_ref, rows_ref):
        me = lax.axis_index("expert")
        core = me % 2
        for chip in range(owners // 2):
            place = pl.ds(chip * tok, tok)
            rows_ref[place, :] = x_ref[block(2 * chip + 1 - core, tok), :]
            rows_ref[pl.ds(half + chip * tok, tok), :] = x_ref[block(2 * chip + core, tok), :]
        other_ref[...] = mxu(rows_ref[:half, :], proj_ref[...]).astype(BF16)
        mine_ref[...] = mxu(rows_ref[half:, :], proj_ref[...]).astype(BF16)

    return local(
        body,
        (shape(half, width), shape(half, width)),
        (x, in_proj),
        "project",
        scratch=[pltpu.VMEM((rows, features), BF16)],
        flops=2 * rows * features * width,
    )


def streams(part, got, out_grad, routing):
    half, width = part.shape
    tok = out_grad.shape[0]
    experts = routing.shape[0]

    def body(part_ref, got_ref, grad_ref, routing_ref, first_ref, second_ref):
        mid, rows = half // 2, tok // 2
        first_ref[:mid, :] = add_bf16(part_ref[:mid, :], got_ref[:mid, :])
        first_ref[mid : mid + experts, :] = routing_ref[...]
        first_ref[mid + experts :, :] = grad_ref[:rows, :]
        second_ref[:mid, :] = add_bf16(part_ref[mid:, :], got_ref[mid:, :])
        second_ref[mid:, :] = grad_ref[rows:, :]

    return local(
        body,
        (shape(half // 2 + experts + tok // 2, width), shape(half // 2 + tok // 2, width)),
        (part, got, out_grad, routing),
        "streams",
    )


def merge(sent, got, sums, flops=0, ties=()):
    width = sent[0].shape[1]
    rows = [value.shape[0] for value in sent]

    def body(*refs):
        count = len(sums)
        for i in range(count):
            sent_ref, got_ref, out_ref = refs[i], refs[count + i], refs[2 * count + i]
            out_ref[: sums[i], :] = add_bf16(sent_ref[: sums[i], :], got_ref[: sums[i], :])
            out_ref[sums[i] : rows[i], :] = sent_ref[sums[i] :, :]
            out_ref[rows[i] :, :] = got_ref[sums[i] :, :]

    return local(
        body,
        tuple(shape(2 * r - s, width) for r, s in zip(rows, sums)),
        tuple(sent) + tuple(got),
        "merge",
        flops=flops,
        ties=ties,
    )


def settle(sent, got, orders, tok, experts, ties=()):
    width = sent[0].shape[1]
    chips = len(orders[0])
    half = chips * tok
    mid, rows = half // 2, tok // 2

    def body(first_ref, second_ref, first_got, second_got, out_ref):
        chip = lax.axis_index("expert") // 2
        out_ref[:mid, :] = add_bf16(first_ref[:mid, :], first_got[:mid, :])
        out_ref[mid:half, :] = add_bf16(second_ref[:mid, :], second_got[:mid, :])
        table = pl.ds(mid, experts)
        out_ref[pl.ds(2 * half, experts), :] = add_bf16(first_ref[table, :], first_got[table, :])
        refs = ((first_ref, first_got, mid + experts), (second_ref, second_got, mid))
        for side, (own, partner, start) in enumerate(refs):
            for place, mask in enumerate(orders[side]):
                src = own if place < chips // 2 else partner
                offset = start + (place % (chips // 2)) * rows
                to = half + pl.multiple_of((chip ^ (mask // 2)) * tok, tok) + side * rows
                out_ref[pl.ds(pl.multiple_of(to, rows), rows), :] = src[pl.ds(offset, rows), :]

    return local(body, shape(2 * half + experts, width), tuple(sent) + tuple(got), "settle", ties=ties)


def experts(mine, other, up_weight, down_weight, half, ties=()):
    local_experts, width, hidden = up_weight.shape
    rows = 2 * half

    def body(mine_ref, other_ref, up, down, act_ref, lat_mine_ref, lat_other_ref, cot):
        me = lax.axis_index("expert")
        all_experts = mine_ref.shape[0] - rows
        ids = lax.broadcasted_iota(jnp.int32, (all_experts, 128), 0)
        slots = lax.broadcasted_iota(jnp.int32, (all_experts, 128), 1)
        pick = jnp.where(ids == slots + me * local_experts, 1.0, 0.0).astype(BF16)
        sources = ((mine_ref, 0), (other_ref, half))
        probs = []
        for src, place in sources:
            cot[pl.ds(place, half), :] = src[half:rows, :]
            probs.append(mxu(src[rows:, :half], pick, TN))
        probs = jnp.concatenate(probs, axis=0)
        total = None
        for i in range(local_experts):
            columns = pl.ds(i * hidden, hidden)
            pre = [mxu(src[:half, :], up[i]) for src, _ in sources]
            positive = jnp.maximum(jnp.concatenate(pre, axis=0), 0.0)
            weighted = positive * probs[:, i : i + 1]
            act_ref[:, columns] = (positive * weighted).astype(BF16)
            grad_act = mxu(cot[...], down[i], NT)
            grad_pre = (grad_act * (2.0 * weighted)).astype(BF16)
            term = mxu(grad_pre, up[i], NT)
            total = term if total is None else total + term
        lat_mine_ref[...] = total[:half].astype(BF16)
        lat_other_ref[...] = total[half:].astype(BF16)

    return local(
        body,
        (shape(rows, local_experts * hidden), shape(half, width), shape(half, width)),
        (mine, other, up_weight, down_weight),
        "experts",
        ties=ties,
        scratch=[pltpu.VMEM((rows, width), BF16)],
        limit=24,
        flops=2 * 3 * rows * width * hidden * local_experts,
    )


def outputs(act, down_weight, half):
    local_experts, hidden, width = down_weight.shape

    def body(act_ref, down, mine_ref, other_ref):
        total = None
        for i in range(local_experts):
            term = mxu(act_ref[:, pl.ds(i * hidden, hidden)], down[i])
            total = term if total is None else total + term
        mine_ref[...] = total[:half].astype(BF16)
        other_ref[...] = total[half:].astype(BF16)

    return local(
        body,
        (shape(half, width), shape(half, width)),
        (act, down_weight),
        "outputs",
        limit=16,
        flops=4 * half * local_experts * hidden * width,
    )


def pieces_of(first, second, chips, ties=()):
    rows, width = first.shape
    tok = rows // chips

    def body(first_ref, second_ref, *out_refs):
        chip = lax.axis_index("expert") // 2
        for mask in range(chips):
            rows = block(chip ^ mask, tok)
            out_refs[mask][...] = add_bf16(first_ref[rows, :], second_ref[rows, :])

    return local(body, tuple(shape(tok, width) for _ in range(chips)), (first, second), "pieces", ties=ties)


def scatter_sum(pieces):
    got = [xor_permute(pieces[k], "expert", 2 * k) for k in range(1, len(pieces))]
    total = pieces[0].astype(F32)
    for piece in got:
        total = total + piece.astype(F32)
    return total.astype(BF16)


def input_grads(pieces, in_proj, tok):
    features, width = in_proj.shape
    rows = len(pieces) * tok

    def body(*refs):
        piece_refs, (proj_ref, out_ref, rows_ref) = refs[: len(pieces)], refs[len(pieces) :]
        me = lax.axis_index("expert")
        for mask, piece_ref in enumerate(piece_refs):
            rows_ref[block(me ^ mask, tok), :] = piece_ref[:tok, :]
        out_ref[...] = mxu(rows_ref[...], proj_ref[...], NT).astype(BF16)

    return local(
        body,
        shape(rows, features),
        tuple(pieces) + (in_proj,),
        "input_grads",
        scratch=[pltpu.VMEM((rows, width), BF16)],
        limit=16,
        flops=2 * rows * features * width,
    )


def arrange(value, hops, chips, tok, tie):
    rows, features = value.shape
    count = 4 if hops else 1
    sources = (value,) + tuple(x for step in hops for x in step)

    def body(*refs):
        x_refs, out_refs = refs[: len(sources)], refs[len(sources) :]
        me = lax.axis_index("expert")

        def place(x_ref, mask):
            for k in range(chips):
                for twin in range(2):
                    out_refs[k][pl.ds((twin * count + mask) * tok, tok), :] = x_ref[
                        block(me ^ (2 * k + twin), tok), :
                    ]

        place(x_refs[0], 0)
        if hops:
            near, middle, middle_far, edge, edge_far = x_refs[1:]
            group = lax.axis_index("dp")
            at_edge = jnp.logical_or(group == 0, group == 3)
            place(near, 1)

            @pl.when(at_edge)
            def _():
                place(edge, 2)
                place(edge_far, 3)

            @pl.when(jnp.logical_not(at_edge))
            def _():
                place(middle_far, 2)
                place(middle, 3)

    out = tuple(shape(2 * count * tok, features) for _ in range(chips))
    return local(body, out, sources, "arrange", ties=(tie,))


def per_device(tokens_x, in_proj, up_weight, down_weight, expert_ids, route_probs, out_grad):
    owners = lax.axis_size("expert")
    groups = lax.axis_size("dp")
    chips = owners // 2
    chip = lax.axis_index("expert") // 2
    tok, top = expert_ids.shape
    all_experts = up_weight.shape[0] * owners
    features, width = in_proj.shape
    half = chips * tok
    bits = [1 << b for b in range(1, owners.bit_length() - 1)]
    gather_groups = groups == 4 and groups * owners * tok * width <= 1 << 22

    chosen = expert_ids[None, :, :] == jnp.arange(all_experts, dtype=jnp.int32)[:, None, None]
    routing = jnp.sum(jnp.where(chosen, route_probs[None, :, :], 0.0), axis=2).astype(BF16)
    routing = lax.dynamic_update_slice(
        jnp.zeros((all_experts, width), BF16), routing, (0, chip * tok)
    )

    part_other, part_mine = project(tokens_x, in_proj, tok)
    got = xor_permute(part_other, "expert", 1)
    sent = streams(part_mine, got, out_grad, routing)
    sums = (half // 2 + all_experts, half // 2)
    hops = line_gather(tokens_x, "dp") if gather_groups else []
    for step, stream_bits in enumerate(zip(bits, bits[::-1])):
        got = [xor_permute(value, "expert", bit) for value, bit in zip(sent, stream_bits)]
        if step + 1 < len(bits):
            sent = merge(sent, got, sums, ties=hop(hops, 0))
    mine = settle(sent, got, (order_of(bits), order_of(bits[::-1])), tok, all_experts, ties=hop(hops, 1))
    other = xor_permute(mine, "expert", 1)
    act, lat_mine, lat_other = experts(mine, other, up_weight, down_weight, half)
    latent_grad = scatter_sum(pieces_of(lat_mine, xor_permute(lat_other, "expert", 1), chips, hop(hops, 2)))
    out_mine, out_other = outputs(act, down_weight, half)
    combined = scatter_sum(pieces_of(out_mine, xor_permute(out_other, "expert", 1), chips))

    held = [latent_grad]
    if gather_groups:
        held += [xor_permute(latent_grad, "dp", m) for m in range(1, groups)]
    own = jnp.concatenate(held, axis=0)
    x_all = arrange(tokens_x, hops, chips, tok, own)
    all_pieces = []
    proj_grad = None
    for k in range(chips):
        piece = own if k == 0 else xor_permute(own, "expert", 2 * k)
        twin = xor_permute(piece, "expert", 1)
        all_pieces += [piece, twin]
        term = mxu(x_all[k], jnp.concatenate([piece, twin], axis=0), TN)
        proj_grad = term if proj_grad is None else proj_grad + term
    input_grad = input_grads(all_pieces, in_proj, tok)
    if not gather_groups:
        proj_grad = lax.psum(proj_grad, "dp")
    return (combined, input_grad, proj_grad)


def solution(mesh):
    return jax.shard_map(
        per_device,
        mesh=mesh,
        in_specs=(
            P("dp", "expert"),
            P("expert", None),
            P("expert", None, None),
            P("expert", None, None),
            P(("dp", "expert"), None),
            P(("dp", "expert"), None),
            P(("dp", "expert"), None),
        ),
        out_specs=(P(("dp", "expert"), None), P("dp", "expert"), P("expert", None)),
        check_vma=False,
    )
```

```python
import jax
import jax.numpy as jnp
from jax import lax
from jax.experimental import pallas as pl
from jax.experimental.pallas import tpu as pltpu
from jax.sharding import PartitionSpec as P

VMEM = pl.BlockSpec(memory_space=pltpu.VMEM)
ANY = pl.BlockSpec(memory_space=pl.ANY)
BF16 = jnp.bfloat16
F32 = jnp.float32
NN = (((1,), (0,)), ((), ()))
NT = (((1,), (1,)), ((), ()))
TN = (((0,), (0,)), ((), ()))
MIB = 1 << 20


def mxu(first, second, dims=NN):
    return lax.dot_general(first, second, dims, preferred_element_type=F32)


def shape(rows, columns, dtype=BF16):
    return jax.ShapeDtypeStruct((rows, columns), dtype)


def add_bf16(first, second):
    return (first.astype(F32) + second.astype(F32)).astype(BF16)


def local(body, outs, args, name, scratch=(), limit=8, flops=0, ties=(), pin=None):
    single = not isinstance(outs, tuple)
    spec = VMEM if pin is None else pl.BlockSpec(memory_space=pin)

    def kernel(*refs):
        body(*refs[: len(args)], *refs[len(args) + len(ties) :])

    if pin is not None:
        args = [pltpu.with_memory_space_constraint(value, pin) for value in args]
    return pl.pallas_call(
        kernel,
        out_shape=outs,
        in_specs=[spec] * len(args) + [ANY] * len(ties),
        out_specs=VMEM if single else tuple(VMEM for _ in outs),
        scratch_shapes=list(scratch),
        compiler_params=pltpu.CompilerParams(vmem_limit_bytes=limit * MIB),
        cost_estimate=pl.CostEstimate(flops=flops, bytes_accessed=MIB, transcendentals=0),
        name=name,
    )(*args, *ties)


def load(value):
    def body(src, dst, sems):
        copies = [
            pltpu.make_async_copy(src.at[i], dst.at[i], sems.at[i]) for i in range(value.shape[0])
        ]
        for copy in copies:
            copy.start()
        for copy in copies:
            copy.wait()

    return local(
        body,
        pltpu.VMEM(value.shape, value.dtype),
        (value,),
        "load",
        scratch=[pltpu.SemaphoreType.DMA((value.shape[0],))],
        pin=pltpu.HBM,
    )


def xor_permute(value, axis, mask):
    size = lax.axis_size(axis)
    return lax.ppermute(value, axis, [(i, i ^ mask) for i in range(size)])


INNER, OUTER = [(1, 2), (2, 1)], [(1, 0), (2, 3)]


def line_gather(value, axis):
    near = xor_permute(value, axis, 1)
    middle = lax.ppermute(value, axis, INNER)
    middle_far = lax.ppermute(near, axis, INNER)
    edge = lax.ppermute(middle, axis, OUTER)
    return [(near, middle), (middle_far, edge)]


def hop(hops, index):
    return hops[index] if index < len(hops) else ()


def order_of(bits):
    masks = [0]
    for bit in bits:
        masks = masks + [mask ^ bit for mask in masks]
    return masks


def block(index, rows):
    return pl.ds(pl.multiple_of(index * rows, rows), rows)


def project(x, in_proj, out_grad, expert_ids, route_probs, all_experts):
    rows, features = x.shape
    width = in_proj.shape[1]
    tok, top = out_grad.shape[0], expert_ids.shape[1]
    chips = rows // tok // 2
    half, mid, cot = rows // 2, rows // 4, tok // 2

    args = (x, in_proj, out_grad, expert_ids.T, route_probs.T)

    def body(*refs):
        other_ref, first_ref, second_ref, rows_ref = refs[5:9]
        x_ref, proj_ref, grad_ref, ids_ref, probs_ref = refs[9:14]
        copies = [
            pltpu.make_async_copy(refs[i], refs[9 + i], refs[14].at[i]) for i in range(len(args))
        ]
        for copy in copies:
            copy.start()
        copies[0].wait()
        me = lax.axis_index("expert")
        core = me % 2
        for chip in range(chips):
            rows_ref[pl.ds(chip * tok, tok), :] = x_ref[block(2 * chip + 1 - core, tok), :]
            rows_ref[pl.ds(half + chip * tok, tok), :] = x_ref[block(2 * chip + core, tok), :]
        copies[1].wait()
        other_ref[...] = mxu(rows_ref[:half, :], proj_ref[...]).astype(BF16)
        mine = mxu(rows_ref[half:, :], proj_ref[...]).astype(BF16)
        first_ref[:mid, :] = mine[:mid]
        second_ref[:mid, :] = mine[mid:]
        for copy in copies[2:]:
            copy.wait()
        names = lax.broadcasted_iota(jnp.int32, (all_experts, tok), 0)
        table = jnp.zeros((all_experts, tok), F32)
        for k in range(top):
            table += jnp.where(names == ids_ref[k : k + 1, :], probs_ref[k : k + 1, :], 0.0)
        token = lax.broadcasted_iota(jnp.int32, (tok, width), 0)
        column = lax.broadcasted_iota(jnp.int32, (tok, width), 1)
        place = jnp.where(column == token + (me // 2) * tok, 1.0, 0.0).astype(BF16)
        first_ref[mid : mid + all_experts, :] = mxu(table.astype(BF16), place).astype(BF16)
        first_ref[mid + all_experts :, :] = grad_ref[:cot, :]
        second_ref[mid:, :] = grad_ref[cot:, :]

    return local(
        body,
        (shape(half, width), shape(mid + all_experts + cot, width), shape(mid + cot, width)),
        args,
        "project",
        scratch=[pltpu.VMEM((rows, features), BF16)]
        + [pltpu.VMEM(value.shape, value.dtype) for value in args]
        + [pltpu.SemaphoreType.DMA((len(args),))],
        pin=pltpu.HBM,
        flops=2 * rows * features * width,
    )


def streams(sent, got, ties=()):
    mid = got.shape[0] // 2

    def body(first_ref, second_ref, got_ref, first_out, second_out):
        for i, (src, dst) in enumerate(((first_ref, first_out), (second_ref, second_out))):
            dst[:mid, :] = add_bf16(src[:mid, :], got_ref[i * mid : (i + 1) * mid, :])
            dst[mid:, :] = src[mid:, :]

    return local(body, tuple(shape(*v.shape) for v in sent), tuple(sent) + (got,), "streams", ties=ties)


def merge(sent, got, sums, ties=()):
    width = sent[0].shape[1]
    rows = [value.shape[0] for value in sent]

    def body(*refs):
        count = len(sums)
        for i in range(count):
            sent_ref, got_ref, out_ref = refs[i], refs[count + i], refs[2 * count + i]
            out_ref[: sums[i], :] = add_bf16(sent_ref[: sums[i], :], got_ref[: sums[i], :])
            out_ref[sums[i] : rows[i], :] = sent_ref[sums[i] :, :]
            out_ref[rows[i] :, :] = got_ref[sums[i] :, :]

    return local(
        body,
        tuple(shape(2 * r - s, width) for r, s in zip(rows, sums)),
        tuple(sent) + tuple(got),
        "merge",
        ties=ties,
    )


def settle(sent, got, orders, tok, experts, ties=()):
    width = sent[0].shape[1]
    chips = len(orders[0])
    half = chips * tok
    mid, rows = half // 2, tok // 2

    def body(first_ref, second_ref, first_got, second_got, out_ref):
        chip = lax.axis_index("expert") // 2
        out_ref[:mid, :] = add_bf16(first_ref[:mid, :], first_got[:mid, :])
        out_ref[mid:half, :] = add_bf16(second_ref[:mid, :], second_got[:mid, :])
        table = pl.ds(mid, experts)
        out_ref[pl.ds(2 * half, experts), :] = add_bf16(first_ref[table, :], first_got[table, :])
        refs = ((first_ref, first_got, mid + experts), (second_ref, second_got, mid))
        for side, (own, partner, start) in enumerate(refs):
            for place, mask in enumerate(orders[side]):
                src = own if place < chips // 2 else partner
                offset = start + (place % (chips // 2)) * rows
                to = half + pl.multiple_of((chip ^ (mask // 2)) * tok, tok) + side * rows
                out_ref[pl.ds(pl.multiple_of(to, rows), rows), :] = src[pl.ds(offset, rows), :]

    return local(body, shape(2 * half + experts, width), tuple(sent) + tuple(got), "settle", ties=ties)


def experts(mine, other, up_weight, down_weight, half, ties=()):
    local_experts, width, hidden = up_weight.shape
    rows = 2 * half

    def body(mine_ref, other_ref, up, down, act_ref, lat_mine_ref, lat_other_ref, cot):
        me = lax.axis_index("expert")
        all_experts = mine_ref.shape[0] - rows
        ids = lax.broadcasted_iota(jnp.int32, (all_experts, 128), 0)
        slots = lax.broadcasted_iota(jnp.int32, (all_experts, 128), 1)
        pick = jnp.where(ids == slots + me * local_experts, 1.0, 0.0).astype(BF16)
        sources = ((mine_ref, 0), (other_ref, half))
        probs = []
        for src, place in sources:
            cot[pl.ds(place, half), :] = src[half:rows, :]
            probs.append(mxu(src[rows:, :half], pick, TN))
        probs = jnp.concatenate(probs, axis=0)
        total = None
        for i in range(local_experts):
            columns = pl.ds(i * hidden, hidden)
            pre = [mxu(src[:half, :], up[i]) for src, _ in sources]
            positive = jnp.maximum(jnp.concatenate(pre, axis=0), 0.0)
            weighted = positive * probs[:, i : i + 1]
            act_ref[:, columns] = (positive * weighted).astype(BF16)
            grad_act = mxu(cot[...], down[i], NT)
            grad_pre = (grad_act * (2.0 * weighted)).astype(BF16)
            term = mxu(grad_pre, up[i], NT)
            total = term if total is None else total + term
        lat_mine_ref[...] = total[:half].astype(BF16)
        lat_other_ref[...] = total[half:].astype(BF16)

    return local(
        body,
        (shape(rows, local_experts * hidden), shape(half, width), shape(half, width)),
        (mine, other, up_weight, down_weight),
        "experts",
        ties=ties,
        scratch=[pltpu.VMEM((rows, width), BF16)],
        limit=24,
        flops=2 * 3 * rows * width * hidden * local_experts,
    )


def outputs(act, down_weight, half):
    local_experts, hidden, width = down_weight.shape

    def body(act_ref, down, mine_ref, other_ref):
        total = None
        for i in range(local_experts):
            term = mxu(act_ref[:, pl.ds(i * hidden, hidden)], down[i])
            total = term if total is None else total + term
        mine_ref[...] = total[:half].astype(BF16)
        other_ref[...] = total[half:].astype(BF16)

    return local(
        body,
        (shape(half, width), shape(half, width)),
        (act, down_weight),
        "outputs",
        limit=16,
        flops=4 * half * local_experts * hidden * width,
    )


def pieces_of(first, second, chips, ties=()):
    rows, width = first.shape
    tok = rows // chips

    def body(first_ref, second_ref, *out_refs):
        chip = lax.axis_index("expert") // 2
        for mask in range(chips):
            rows = block(chip ^ mask, tok)
            out_refs[mask][...] = add_bf16(first_ref[rows, :], second_ref[rows, :])

    return local(body, tuple(shape(tok, width) for _ in range(chips)), (first, second), "pieces", ties=ties)


def scatter(pieces):
    return [xor_permute(pieces[k], "expert", 2 * k) for k in range(1, len(pieces))]


def add_pieces(pieces, start=0, ties=()):
    rows, width = pieces[0].shape

    def body(*refs):
        total = refs[0][...].astype(F32)
        for ref in refs[1:-1]:
            total = total + ref[pl.ds(start, rows), :].astype(F32)
        refs[-1][...] = total.astype(BF16)

    return local(body, shape(rows, width), tuple(pieces), "add_pieces", ties=ties)


def head(value, tails, ties=()):
    rows, width = value.shape
    count = len(tails)

    def body(*refs):
        for tail, out in zip(refs[1 : 1 + count], refs[1 + count :]):
            out[pl.ds(0, rows), :] = refs[0][...]
            out[pl.ds(rows, tail.shape[0]), :] = tail[...]

    outs = tuple(shape(rows + tail.shape[0], width) for tail in tails)
    return local(body, outs, (value, *tails), "head", ties=ties)


def stack(values, rows, ties=(), flops=0):
    width = values[0].shape[1]

    def body(*refs):
        for i, ref in enumerate(refs[:-1]):
            refs[-1][pl.ds(i * rows, rows), :] = ref[pl.ds(0, rows), :]

    return local(body, shape(len(values) * rows, width), tuple(values), "stack", ties=ties, flops=flops)


def input_grads(near, twins, in_proj, tok):
    features, width = in_proj.shape
    rows = 2 * near.shape[0]

    def body(near_ref, twins_ref, proj_ref, out_ref, rows_ref):
        me = lax.axis_index("expert")
        for mask in range(rows // tok):
            src = (near_ref, twins_ref)[mask % 2]
            rows_ref[block(me ^ mask, tok), :] = src[pl.ds(mask // 2 * tok, tok), :]
        out_ref[...] = mxu(rows_ref[...], proj_ref[...], NT).astype(BF16)

    return local(
        body,
        shape(rows, features),
        (near, twins, in_proj),
        "input_grads",
        scratch=[pltpu.VMEM((rows, width), BF16)],
        limit=16,
        flops=2 * rows * features * width,
    )


def arrange(value, hops, chips, tok, tie):
    rows, features = value.shape
    count = 4 if hops else 1
    sources = (value,) + tuple(x for step in hops for x in step)

    def body(*refs):
        x_refs, out_refs = refs[: len(sources)], refs[len(sources) :]
        me = lax.axis_index("expert")

        def place(x_ref, mask):
            for k in range(chips):
                for twin in range(2):
                    out_refs[k][pl.ds((twin * count + mask) * tok, tok), :] = x_ref[
                        block(me ^ (2 * k + twin), tok), :
                    ]

        place(x_refs[0], 0)
        if hops:
            near, middle, middle_far, edge, edge_far = x_refs[1:]
            group = lax.axis_index("dp")
            at_edge = jnp.logical_or(group == 0, group == 3)
            place(near, 1)

            @pl.when(at_edge)
            def _():
                place(edge, 2)
                place(edge_far, 3)

            @pl.when(jnp.logical_not(at_edge))
            def _():
                place(middle_far, 2)
                place(middle, 3)

    out = tuple(shape(2 * count * tok, features) for _ in range(chips))
    return local(body, out, sources, "arrange", ties=(tie,))


def proj_round(x_rows, near, far, chip, tok, before, last):
    rows, features = x_rows.shape
    width = near[0].shape[1]
    given = [x_rows, *near, *far] + ([] if before is None else [before])
    steps = 4 if features % 512 == 0 else 1
    tile = features // steps

    def body(*refs):
        x_ref = refs[0]
        out_ref, rows_ref = refs[len(given)], refs[len(given) + 1]
        for twin in range(2):
            start = twin * (rows // 2)
            rows_ref[pl.ds(start, tok), :] = refs[1 + twin][pl.ds(chip * tok, tok), :]
            if far:
                rows_ref[pl.ds(start + tok, rows // 2 - tok), :] = refs[3 + twin][...]
        copies = []
        for i in range(steps):
            part = pl.ds(i * tile, tile)
            total = mxu(x_ref[:, part], rows_ref[...], TN)
            if before is not None:
                total = total + refs[len(given) - 1][part, :]
            if last:
                whole_ref, sems = refs[len(given) + 2], refs[len(given) + 3]
                whole_ref[part, :] = total
                copies.append(pltpu.make_async_copy(whole_ref.at[part], out_ref.at[part], sems.at[i]))
                copies[-1].start()
            else:
                out_ref[part, :] = total
        for copy in copies:
            copy.wait()

    scratch = [pltpu.VMEM((rows, width), BF16)]
    if last:
        scratch += [pltpu.VMEM((features, width), F32), pltpu.SemaphoreType.DMA((steps,))]
    return pl.pallas_call(
        body,
        out_shape=shape(features, width, F32),
        in_specs=[VMEM] * len(given),
        out_specs=ANY if last else VMEM,
        scratch_shapes=scratch,
        compiler_params=pltpu.CompilerParams(vmem_limit_bytes=16 * MIB),
        cost_estimate=pl.CostEstimate(
            flops=2 * rows * features * width, bytes_accessed=4 * MIB, transcendentals=0
        ),
        name="proj_round",
    )(*given)


def per_device(tokens_x, in_proj, up_weight, down_weight, expert_ids, route_probs, out_grad):
    owners = lax.axis_size("expert")
    groups = lax.axis_size("dp")
    chips = owners // 2
    chip = lax.axis_index("expert") // 2
    tok, top = expert_ids.shape
    all_experts = up_weight.shape[0] * owners
    features, width = in_proj.shape
    half = chips * tok
    bits = [1 << b for b in range(1, owners.bit_length() - 1)]
    gather_groups = groups == 4 and groups * owners * tok * width <= 1 << 22

    part_other, *sent = project(tokens_x, in_proj, out_grad, expert_ids, route_probs, all_experts)
    sums = (half // 2 + all_experts, half // 2)
    hops = line_gather(tokens_x, "dp") if gather_groups else []
    last = [lax.ppermute(hops[1][0], "dp", OUTER)] if hops else []
    up, down = load(up_weight), load(down_weight)
    sent = streams(sent, xor_permute(part_other, "expert", 1))
    for step, stream_bits in enumerate(zip(bits, bits[::-1])):
        got = [xor_permute(value, "expert", bit) for value, bit in zip(sent, stream_bits)]
        if step + 1 < len(bits):
            sent = merge(sent, got, sums)
    mine = settle(sent, got, (order_of(bits), order_of(bits[::-1])), tok, all_experts, ties=(up, down, *hop(hops, 0)))
    other = xor_permute(mine, "expert", 1)

    act, lat_mine, lat_other = experts(mine, other, up, down, half)
    out_mine, out_other = outputs(act, down, half)
    out_pieces = pieces_of(out_mine, xor_permute(out_other, "expert", 1), chips)
    lat_pieces = pieces_of(lat_mine, xor_permute(lat_other, "expert", 1), chips)
    got = scatter(lat_pieces)
    latent_grad = add_pieces((lat_pieces[0], *got), ties=hop(hops, 1))

    own = ()
    if gather_groups:
        across = [xor_permute(latent_grad, "dp", m) for m in range(1, groups)]
        own = stack(across, tok, ties=last)
        hops.append(tuple(last))
    after = (own,) if gather_groups else ()
    sent = head(latent_grad, out_pieces[1:])
    got = scatter([None, *sent])
    combined = add_pieces((out_pieces[0], *got), tok, ties=after)
    near = stack([latent_grad, *got], tok, ties=after)
    split = near.shape[0] // 2
    twins = [xor_permute(v, "expert", 1) for v in (near[:split], near[split:])]
    twins = jnp.concatenate(twins, axis=0)
    input_grad = input_grads(near, twins, in_proj, tok)
    far = [() for _ in range(chips)]
    x_all = arrange(tokens_x, hops, chips, tok, latent_grad)
    order = [0] + list(range(chips - 1, 0, -1))
    if gather_groups:
        far[0] = (own, xor_permute(own, "expert", 1))
    proj_grad = proj_round(x_all[0], (near, twins), far[0], 0, tok, None, False)
    if gather_groups:
        ties = (proj_grad, input_grad, combined)
        for k in order[1:]:
            piece = xor_permute(own, "expert", 2 * k)
            relay = stack([piece], piece.shape[0], ties)
            far[k] = (relay, xor_permute(relay, "expert", 1))
            ties = ()
    for k in order[1:]:
        proj_grad = proj_round(x_all[k], (near, twins), far[k], k, tok, proj_grad, k == order[-1])
    if not gather_groups:
        proj_grad = lax.psum(proj_grad, "dp")
    return (combined, input_grad, proj_grad)


def solution(mesh):
    return jax.shard_map(
        per_device,
        mesh=mesh,
        in_specs=(
            P("dp", "expert"),
            P("expert", None),
            P("expert", None, None),
            P("expert", None, None),
            P(("dp", "expert"), None),
            P(("dp", "expert"), None),
            P(("dp", "expert"), None),
        ),
        out_specs=(P(("dp", "expert"), None), P("dp", "expert"), P("expert", None)),
        check_vma=False,
    )
```

```python
import jax
import jax.numpy as jnp
from jax import lax
from jax.experimental import pallas as pl
from jax.experimental.pallas import tpu as pltpu
from jax.sharding import PartitionSpec as P

VMEM = pl.BlockSpec(memory_space=pltpu.VMEM)
ANY = pl.BlockSpec(memory_space=pl.ANY)
BF16 = jnp.bfloat16
F32 = jnp.float32
NN = (((1,), (0,)), ((), ()))
NT = (((1,), (1,)), ((), ()))
TN = (((0,), (0,)), ((), ()))
MIB = 1 << 20


def mxu(first, second, dims=NN):
    return lax.dot_general(first, second, dims, preferred_element_type=F32)


def shape(rows, columns, dtype=BF16):
    return jax.ShapeDtypeStruct((rows, columns), dtype)


def add_bf16(first, second):
    return (first.astype(F32) + second.astype(F32)).astype(BF16)


def local(body, outs, args, name, scratch=(), limit=8, flops=0, ties=(), pin=None):
    single = not isinstance(outs, tuple)
    spec = VMEM if pin is None else pl.BlockSpec(memory_space=pin)

    def kernel(*refs):
        body(*refs[: len(args)], *refs[len(args) + len(ties) :])

    if pin is not None:
        args = [pltpu.with_memory_space_constraint(value, pin) for value in args]
    return pl.pallas_call(
        kernel,
        out_shape=outs,
        in_specs=[spec] * len(args) + [ANY] * len(ties),
        out_specs=VMEM if single else tuple(VMEM for _ in outs),
        scratch_shapes=list(scratch),
        compiler_params=pltpu.CompilerParams(vmem_limit_bytes=limit * MIB),
        cost_estimate=pl.CostEstimate(flops=flops, bytes_accessed=MIB, transcendentals=0),
        name=name,
    )(*args, *ties)


def load(*values):
    count = len(values)
    parts = [(j, i) for i in range(values[0].shape[0]) for j in range(count)]

    def body(*refs):
        copies = [
            pltpu.make_async_copy(refs[j].at[i], refs[count + j].at[i], refs[2 * count].at[place])
            for place, (j, i) in enumerate(parts)
        ]
        for copy in copies:
            copy.start()
        for copy in copies:
            copy.wait()

    return local(
        body,
        tuple(pltpu.VMEM(value.shape, value.dtype) for value in values),
        values,
        "load",
        scratch=[pltpu.SemaphoreType.DMA((len(parts),))],
        pin=pltpu.HBM,
    )


def xor_permute(value, axis, mask):
    size = lax.axis_size(axis)
    return lax.ppermute(value, axis, [(i, i ^ mask) for i in range(size)])


INNER, OUTER = [(1, 2), (2, 1)], [(1, 0), (2, 3)]


def line_gather(value, axis):
    near = xor_permute(value, axis, 1)
    middle = lax.ppermute(value, axis, INNER)
    middle_far = lax.ppermute(near, axis, INNER)
    edge = lax.ppermute(middle, axis, OUTER)
    return [(near, middle), (middle_far, edge)]


def hops_last(hops):
    if not hops:
        return ()
    value = hops[1][0]
    rows = value.shape[0] // 2
    return tuple(lax.ppermute(value[i * rows : (i + 1) * rows], "dp", OUTER) for i in range(2))


def hop(hops, index):
    return hops[index] if index < len(hops) else ()


def order_of(bits):
    masks = [0]
    for bit in bits:
        masks = masks + [mask ^ bit for mask in masks]
    return masks


def block(index, rows):
    return pl.ds(pl.multiple_of(index * rows, rows), rows)


def project(x, in_proj, out_grad, expert_ids, route_probs, all_experts):
    rows, features = x.shape
    width = in_proj.shape[1]
    tok, top = out_grad.shape[0], expert_ids.shape[1]
    chips = rows // tok // 2
    half, mid, cot = rows // 2, rows // 4, tok // 2

    args = (x, in_proj, out_grad, expert_ids.T, route_probs.T)

    def body(*refs):
        other_ref, first_ref, second_ref, rows_ref = refs[5:9]
        x_ref, proj_ref, grad_ref, ids_ref, probs_ref = refs[9:14]
        copies = [
            pltpu.make_async_copy(refs[i], refs[9 + i], refs[14].at[i]) for i in range(len(args))
        ]
        for copy in copies:
            copy.start()
        copies[0].wait()
        me = lax.axis_index("expert")
        core = me % 2
        for chip in range(chips):
            rows_ref[pl.ds(chip * tok, tok), :] = x_ref[block(2 * chip + 1 - core, tok), :]
            rows_ref[pl.ds(half + chip * tok, tok), :] = x_ref[block(2 * chip + core, tok), :]
        copies[1].wait()
        other_ref[...] = mxu(rows_ref[:half, :], proj_ref[...]).astype(BF16)
        mine = mxu(rows_ref[half:, :], proj_ref[...]).astype(BF16)
        first_ref[:mid, :] = mine[:mid]
        second_ref[:mid, :] = mine[mid:]
        for copy in copies[2:]:
            copy.wait()
        names = lax.broadcasted_iota(jnp.int32, (all_experts, tok), 0)
        table = jnp.zeros((all_experts, tok), F32)
        for k in range(top):
            table += jnp.where(names == ids_ref[k : k + 1, :], probs_ref[k : k + 1, :], 0.0)
        token = lax.broadcasted_iota(jnp.int32, (tok, width), 0)
        column = lax.broadcasted_iota(jnp.int32, (tok, width), 1)
        place = jnp.where(column == token + (me // 2) * tok, 1.0, 0.0).astype(BF16)
        first_ref[mid : mid + all_experts, :] = mxu(table.astype(BF16), place).astype(BF16)
        first_ref[mid + all_experts :, :] = grad_ref[:cot, :]
        second_ref[mid:, :] = grad_ref[cot:, :]

    return local(
        body,
        (shape(half, width), shape(mid + all_experts + cot, width), shape(mid + cot, width)),
        args,
        "project",
        scratch=[pltpu.VMEM((rows, features), BF16)]
        + [pltpu.VMEM(value.shape, value.dtype) for value in args]
        + [pltpu.SemaphoreType.DMA((len(args),))],
        pin=pltpu.HBM,
        flops=2 * rows * features * width,
    )


def streams(sent, got, ties=()):
    mid = got.shape[0] // 2

    def body(first_ref, second_ref, got_ref, first_out, second_out):
        for i, (src, dst) in enumerate(((first_ref, first_out), (second_ref, second_out))):
            dst[:mid, :] = add_bf16(src[:mid, :], got_ref[i * mid : (i + 1) * mid, :])
            dst[mid:, :] = src[mid:, :]

    return local(body, tuple(shape(*v.shape) for v in sent), tuple(sent) + (got,), "streams", ties=ties)


def merge(sent, got, sums, ties=()):
    width = sent[0].shape[1]
    rows = [value.shape[0] for value in sent]

    def body(*refs):
        count = len(sums)
        for i in range(count):
            sent_ref, got_ref, out_ref = refs[i], refs[count + i], refs[2 * count + i]
            out_ref[: sums[i], :] = add_bf16(sent_ref[: sums[i], :], got_ref[: sums[i], :])
            out_ref[sums[i] : rows[i], :] = sent_ref[sums[i] :, :]
            out_ref[rows[i] :, :] = got_ref[sums[i] :, :]

    return local(
        body,
        tuple(shape(2 * r - s, width) for r, s in zip(rows, sums)),
        tuple(sent) + tuple(got),
        "merge",
        ties=ties,
    )


def settle(sent, got, orders, tok, experts, ties=()):
    width = sent[0].shape[1]
    chips = len(orders[0])
    half = chips * tok
    mid, rows = half // 2, tok // 2

    def body(first_ref, second_ref, first_got, second_got, out_ref):
        chip = lax.axis_index("expert") // 2
        out_ref[:mid, :] = add_bf16(first_ref[:mid, :], first_got[:mid, :])
        out_ref[mid:half, :] = add_bf16(second_ref[:mid, :], second_got[:mid, :])
        table = pl.ds(mid, experts)
        out_ref[pl.ds(2 * half, experts), :] = add_bf16(first_ref[table, :], first_got[table, :])
        refs = ((first_ref, first_got, mid + experts), (second_ref, second_got, mid))
        for side, (own, partner, start) in enumerate(refs):
            for place, mask in enumerate(orders[side]):
                src = own if place < chips // 2 else partner
                offset = start + (place % (chips // 2)) * rows
                to = half + pl.multiple_of((chip ^ (mask // 2)) * tok, tok) + side * rows
                out_ref[pl.ds(pl.multiple_of(to, rows), rows), :] = src[pl.ds(offset, rows), :]

    return local(body, shape(2 * half + experts, width), tuple(sent) + tuple(got), "settle", ties=ties)


def preacts(latent, up_weight, rows):
    local_experts, width, hidden = up_weight.shape

    def body(latent_ref, up, out_ref):
        for i in range(local_experts):
            out_ref[:, pl.ds(i * hidden, hidden)] = jnp.maximum(mxu(latent_ref[:rows, :], up[i]), 0.0)

    return local(
        body,
        shape(rows, local_experts * hidden, F32),
        (latent, up_weight),
        "preacts",
        limit=16,
        flops=2 * rows * width * hidden * local_experts,
    )


def experts(positive, mine, other, up_weight, down_weight):
    local_experts, width, hidden = up_weight.shape
    half = positive.shape[0]
    rows = 2 * half

    def body(positive_ref, mine_ref, other_ref, up, down, act_ref, lat_mine_ref, lat_other_ref, cot):
        me = lax.axis_index("expert")
        all_experts = mine_ref.shape[0] - rows
        ids = lax.broadcasted_iota(jnp.int32, (all_experts, 128), 0)
        slots = lax.broadcasted_iota(jnp.int32, (all_experts, 128), 1)
        pick = jnp.where(ids == slots + me * local_experts, 1.0, 0.0).astype(BF16)
        probs = []
        for src, place in ((mine_ref, 0), (other_ref, half)):
            cot[pl.ds(place, half), :] = src[half:rows, :]
            probs.append(mxu(src[rows:, :half], pick, TN))
        probs = jnp.concatenate(probs, axis=0)
        total = None
        for i in range(local_experts):
            columns = pl.ds(i * hidden, hidden)
            other = jnp.maximum(mxu(other_ref[:half, :], up[i]), 0.0)
            positive = jnp.concatenate([positive_ref[:, columns], other], axis=0)
            weighted = positive * probs[:, i : i + 1]
            act_ref[:, columns] = (positive * weighted).astype(BF16)
            grad_act = mxu(cot[...], down[i], NT)
            grad_pre = (grad_act * (2.0 * weighted)).astype(BF16)
            term = mxu(grad_pre, up[i], NT)
            total = term if total is None else total + term
        lat_mine_ref[...] = total[:half].astype(BF16)
        lat_other_ref[...] = total[half:].astype(BF16)

    return local(
        body,
        (shape(rows, local_experts * hidden), shape(half, width), shape(half, width)),
        (positive, mine, other, up_weight, down_weight),
        "experts",
        scratch=[pltpu.VMEM((rows, width), BF16)],
        limit=24,
        flops=2 * 5 * half * width * hidden * local_experts,
    )


def outputs(act, down_weight, half):
    local_experts, hidden, width = down_weight.shape

    def body(act_ref, down, mine_ref, other_ref):
        total = None
        for i in range(local_experts):
            term = mxu(act_ref[:, pl.ds(i * hidden, hidden)], down[i])
            total = term if total is None else total + term
        mine_ref[...] = total[:half].astype(BF16)
        other_ref[...] = total[half:].astype(BF16)

    return local(
        body,
        (shape(half, width), shape(half, width)),
        (act, down_weight),
        "outputs",
        limit=16,
        flops=4 * half * local_experts * hidden * width,
    )


def pieces_of(first, second, chips, ties=()):
    rows, width = first.shape
    tok = rows // chips

    def body(first_ref, second_ref, *out_refs):
        chip = lax.axis_index("expert") // 2
        for mask in range(chips):
            rows = block(chip ^ mask, tok)
            out_refs[mask][...] = add_bf16(first_ref[rows, :], second_ref[rows, :])

    return local(body, tuple(shape(tok, width) for _ in range(chips)), (first, second), "pieces", ties=ties)


def scatter(pieces):
    return [xor_permute(pieces[k], "expert", 2 * k) for k in range(1, len(pieces))]


def add_pieces(pieces, start=0, ties=()):
    rows, width = pieces[0].shape

    def body(*refs):
        total = refs[0][...].astype(F32)
        for ref in refs[1:-1]:
            total = total + ref[pl.ds(start, rows), :].astype(F32)
        refs[-1][...] = total.astype(BF16)

    return local(body, shape(rows, width), tuple(pieces), "add_pieces", ties=ties)


def head(value, tails, ties=()):
    rows, width = value.shape
    count = len(tails)

    def body(*refs):
        for tail, out in zip(refs[1 : 1 + count], refs[1 + count :]):
            out[pl.ds(0, rows), :] = refs[0][...]
            out[pl.ds(rows, tail.shape[0]), :] = tail[...]

    outs = tuple(shape(rows + tail.shape[0], width) for tail in tails)
    return local(body, outs, (value, *tails), "head", ties=ties)


def stack(values, rows, ties=(), flops=0):
    width = values[0].shape[1]

    def body(*refs):
        for i, ref in enumerate(refs[:-1]):
            refs[-1][pl.ds(i * rows, rows), :] = ref[pl.ds(0, rows), :]

    return local(body, shape(len(values) * rows, width), tuple(values), "stack", ties=ties, flops=flops)


def input_grads(near, twins, in_proj, tok):
    features, width = in_proj.shape
    rows = 2 * near.shape[0]

    def body(near_ref, twins_ref, proj_ref, out_ref, rows_ref):
        me = lax.axis_index("expert")
        for mask in range(rows // tok):
            src = (near_ref, twins_ref)[mask % 2]
            rows_ref[block(me ^ mask, tok), :] = src[pl.ds(mask // 2 * tok, tok), :]
        out_ref[...] = mxu(rows_ref[...], proj_ref[...], NT).astype(BF16)

    return local(
        body,
        shape(rows, features),
        (near, twins, in_proj),
        "input_grads",
        scratch=[pltpu.VMEM((rows, width), BF16)],
        limit=16,
        flops=2 * rows * features * width,
    )


def arrange(value, hops, chips, tok, tie):
    rows, features = value.shape
    count = 4 if hops else 1
    sources = (value,) + tuple(x for step in hops for x in step)

    def body(*refs):
        x_refs, out_refs = refs[: len(sources)], refs[len(sources) :]
        me = lax.axis_index("expert")

        def place(x_ref, mask):
            for k in range(chips):
                for twin in range(2):
                    out_refs[k][pl.ds((twin * count + mask) * tok, tok), :] = x_ref[
                        block(me ^ (2 * k + twin), tok), :
                    ]

        place(x_refs[0], 0)
        if hops:
            near, middle, middle_far, edge, edge_far = x_refs[1:]
            group = lax.axis_index("dp")
            at_edge = jnp.logical_or(group == 0, group == 3)
            place(near, 1)

            @pl.when(at_edge)
            def _():
                place(edge, 2)
                place(edge_far, 3)

            @pl.when(jnp.logical_not(at_edge))
            def _():
                place(middle_far, 2)
                place(middle, 3)

    out = tuple(shape(2 * count * tok, features) for _ in range(chips))
    return local(body, out, sources, "arrange", ties=(tie,))


def proj_round(x_rows, near, far, chip, tok, before, last):
    rows, features = x_rows.shape
    width = near[0].shape[1]
    given = [x_rows, *near, *far] + ([] if before is None else [before])
    steps = 4 if features % 512 == 0 else 1
    tile = features // steps

    def body(*refs):
        x_ref = refs[0]
        out_ref, rows_ref = refs[len(given)], refs[len(given) + 1]
        for twin in range(2):
            start = twin * (rows // 2)
            rows_ref[pl.ds(start, tok), :] = refs[1 + twin][pl.ds(chip * tok, tok), :]
            if far:
                rows_ref[pl.ds(start + tok, rows // 2 - tok), :] = refs[3 + twin][...]
        copies = []
        for i in range(steps):
            part = pl.ds(i * tile, tile)
            total = mxu(x_ref[:, part], rows_ref[...], TN)
            if before is not None:
                total = total + refs[len(given) - 1][part, :]
            if last:
                whole_ref, sems = refs[len(given) + 2], refs[len(given) + 3]
                whole_ref[part, :] = total
                copies.append(pltpu.make_async_copy(whole_ref.at[part], out_ref.at[part], sems.at[i]))
                copies[-1].start()
            else:
                out_ref[part, :] = total
        for copy in copies:
            copy.wait()

    scratch = [pltpu.VMEM((rows, width), BF16)]
    if last:
        scratch += [pltpu.VMEM((features, width), F32), pltpu.SemaphoreType.DMA((steps,))]
    return pl.pallas_call(
        body,
        out_shape=shape(features, width, F32),
        in_specs=[VMEM] * len(given),
        out_specs=ANY if last else VMEM,
        scratch_shapes=scratch,
        compiler_params=pltpu.CompilerParams(vmem_limit_bytes=16 * MIB),
        cost_estimate=pl.CostEstimate(
            flops=2 * rows * features * width, bytes_accessed=4 * MIB, transcendentals=0
        ),
        name="proj_round",
    )(*given)


def per_device(tokens_x, in_proj, up_weight, down_weight, expert_ids, route_probs, out_grad):
    owners = lax.axis_size("expert")
    groups = lax.axis_size("dp")
    chips = owners // 2
    chip = lax.axis_index("expert") // 2
    tok, top = expert_ids.shape
    all_experts = up_weight.shape[0] * owners
    features, width = in_proj.shape
    half = chips * tok
    bits = [1 << b for b in range(1, owners.bit_length() - 1)]
    gather_groups = groups == 4 and groups * owners * tok * width <= 1 << 22

    part_other, *sent = project(tokens_x, in_proj, out_grad, expert_ids, route_probs, all_experts)
    sums = (half // 2 + all_experts, half // 2)
    hops = line_gather(tokens_x, "dp") if gather_groups else []
    last = hops_last(hops)
    up, down = load(up_weight, down_weight)
    sent = streams(sent, xor_permute(part_other, "expert", 1))
    for step, stream_bits in enumerate(zip(bits, bits[::-1])):
        got = [xor_permute(value, "expert", bit) for value, bit in zip(sent, stream_bits)]
        if step + 1 < len(bits):
            sent = merge(sent, got, sums)
    mine = settle(sent, got, (order_of(bits), order_of(bits[::-1])), tok, all_experts, ties=(up, down, *hop(hops, 0)))
    other = xor_permute(mine, "expert", 1)

    positive = preacts(mine, up, half)
    act, lat_mine, lat_other = experts(positive, mine, other, up, down)
    out_mine, out_other = outputs(act, down, half)
    out_pieces = pieces_of(out_mine, xor_permute(out_other, "expert", 1), chips)
    lat_pieces = pieces_of(lat_mine, xor_permute(lat_other, "expert", 1), chips)
    got = scatter(lat_pieces)
    latent_grad = add_pieces((lat_pieces[0], *got), ties=hop(hops, 1))

    own = ()
    if gather_groups:
        across = [xor_permute(latent_grad, "dp", m) for m in range(1, groups)]
        own = stack(across, tok, ties=last)
        hops.append((jnp.concatenate(last, axis=0),))
    after = (own,) if gather_groups else ()
    sent = head(latent_grad, out_pieces[1:])
    got = scatter([None, *sent])
    combined = add_pieces((out_pieces[0], *got), tok, ties=after)
    near = stack([latent_grad, *got], tok, ties=after)
    split = near.shape[0] // 2
    twins = [xor_permute(v, "expert", 1) for v in (near[:split], near[split:])]
    twins = jnp.concatenate(twins, axis=0)
    input_grad = input_grads(near, twins, in_proj, tok)
    far = [() for _ in range(chips)]
    x_all = arrange(tokens_x, hops, chips, tok, latent_grad)
    order = [0] + list(range(chips - 1, 0, -1))
    if gather_groups:
        far[0] = (own, xor_permute(own, "expert", 1))
    proj_grad = proj_round(x_all[0], (near, twins), far[0], 0, tok, None, False)
    if gather_groups:
        pieces = {k: xor_permute(own, "expert", 2 * k) for k in order[1:]}
        for k in order[1:]:
            if k == order[-1]:
                ties = (proj_grad, input_grad, combined)
            else:
                ties = (pieces[order[-1]],) if k == order[-2] else ()
            relay = stack([pieces[k]], pieces[k].shape[0], ties)
            far[k] = (relay, xor_permute(relay, "expert", 1))
    for k in order[1:]:
        proj_grad = proj_round(x_all[k], (near, twins), far[k], k, tok, proj_grad, k == order[-1])
    if not gather_groups:
        proj_grad = lax.psum(proj_grad, "dp")
    return (combined, input_grad, proj_grad)


def solution(mesh):
    return jax.shard_map(
        per_device,
        mesh=mesh,
        in_specs=(
            P("dp", "expert"),
            P("expert", None),
            P("expert", None, None),
            P("expert", None, None),
            P(("dp", "expert"), None),
            P(("dp", "expert"), None),
            P(("dp", "expert"), None),
        ),
        out_specs=(P(("dp", "expert"), None), P("dp", "expert"), P("expert", None)),
        check_vma=False,
    )
```

```python
import jax
import jax.numpy as jnp
from jax import lax
from jax.experimental import pallas as pl
from jax.experimental.pallas import tpu as pltpu
from jax.sharding import PartitionSpec as P

VMEM = pl.BlockSpec(memory_space=pltpu.VMEM)
ANY = pl.BlockSpec(memory_space=pl.ANY)
BF16 = jnp.bfloat16
F32 = jnp.float32
NN = (((1,), (0,)), ((), ()))
NT = (((1,), (1,)), ((), ()))
TN = (((0,), (0,)), ((), ()))
MIB = 1 << 20


def mxu(first, second, dims=NN):
    return lax.dot_general(first, second, dims, preferred_element_type=F32)


def shape(rows, columns, dtype=BF16):
    return jax.ShapeDtypeStruct((rows, columns), dtype)


def add_bf16(first, second):
    return (first.astype(F32) + second.astype(F32)).astype(BF16)


def local(body, outs, args, name, scratch=(), limit=8, flops=0, ties=(), pin=None):
    single = not isinstance(outs, tuple)
    spec = VMEM if pin is None else pl.BlockSpec(memory_space=pin)

    def kernel(*refs):
        body(*refs[: len(args)], *refs[len(args) + len(ties) :])

    if pin is not None:
        args = [pltpu.with_memory_space_constraint(value, pin) for value in args]
    return pl.pallas_call(
        kernel,
        out_shape=outs,
        in_specs=[spec] * len(args) + [ANY] * len(ties),
        out_specs=VMEM if single else tuple(VMEM for _ in outs),
        scratch_shapes=list(scratch),
        compiler_params=pltpu.CompilerParams(vmem_limit_bytes=limit * MIB),
        cost_estimate=pl.CostEstimate(flops=flops, bytes_accessed=MIB, transcendentals=0),
        name=name,
    )(*args, *ties)


def load(*values):
    count = len(values)
    parts = [(j, i) for i in range(values[0].shape[0]) for j in range(count)]

    def body(*refs):
        copies = [
            pltpu.make_async_copy(refs[j].at[i], refs[count + j].at[i], refs[2 * count].at[place])
            for place, (j, i) in enumerate(parts)
        ]
        for copy in copies:
            copy.start()
        for copy in copies:
            copy.wait()

    return local(
        body,
        tuple(pltpu.VMEM(value.shape, value.dtype) for value in values),
        values,
        "load",
        scratch=[pltpu.SemaphoreType.DMA((len(parts),))],
        pin=pltpu.HBM,
    )


def xor_permute(value, axis, mask):
    size = lax.axis_size(axis)
    return lax.ppermute(value, axis, [(i, i ^ mask) for i in range(size)])


def order_of(bits):
    masks = [0]
    for bit in bits:
        masks = masks + [mask ^ bit for mask in masks]
    return masks


def block(index, rows):
    return pl.ds(pl.multiple_of(index * rows, rows), rows)


def project(x, in_proj, out_grad, expert_ids, route_probs, all_experts):
    rows, features = x.shape
    width = in_proj.shape[1]
    tok, top = out_grad.shape[0], expert_ids.shape[1]
    chips = rows // tok // 2
    half, mid, cot = rows // 2, rows // 4, tok // 2

    args = (x, in_proj, out_grad, expert_ids.T, route_probs.T)

    def body(*refs):
        other_ref, first_ref, second_ref, x_ref, rows_ref = refs[5:10]
        proj_ref, grad_ref, ids_ref, probs_ref = refs[10:14]
        held = (x_ref, proj_ref, grad_ref, ids_ref, probs_ref)
        copies = [
            pltpu.make_async_copy(refs[i], held[i], refs[14].at[i]) for i in range(len(args))
        ]
        for copy in copies:
            copy.start()
        copies[0].wait()
        me = lax.axis_index("expert")
        core = me % 2
        for chip in range(chips):
            rows_ref[pl.ds(chip * tok, tok), :] = x_ref[block(2 * chip + 1 - core, tok), :]
            rows_ref[pl.ds(half + chip * tok, tok), :] = x_ref[block(2 * chip + core, tok), :]
        copies[1].wait()
        other_ref[...] = mxu(rows_ref[:half, :], proj_ref[...]).astype(BF16)
        mine = mxu(rows_ref[half:, :], proj_ref[...]).astype(BF16)
        first_ref[:mid, :] = mine[:mid]
        second_ref[:mid, :] = mine[mid:]
        for copy in copies[2:]:
            copy.wait()
        names = lax.broadcasted_iota(jnp.int32, (all_experts, tok), 0)
        table = jnp.zeros((all_experts, tok), F32)
        for k in range(top):
            table += jnp.where(names == ids_ref[k : k + 1, :], probs_ref[k : k + 1, :], 0.0)
        token = lax.broadcasted_iota(jnp.int32, (tok, width), 0)
        column = lax.broadcasted_iota(jnp.int32, (tok, width), 1)
        place = jnp.where(column == token + (me // 2) * tok, 1.0, 0.0).astype(BF16)
        first_ref[mid : mid + all_experts, :] = mxu(table.astype(BF16), place).astype(BF16)
        first_ref[mid + all_experts :, :] = grad_ref[:cot, :]
        second_ref[mid:, :] = grad_ref[cot:, :]

    return local(
        body,
        (
            shape(half, width),
            shape(mid + all_experts + cot, width),
            shape(mid + cot, width),
            pltpu.VMEM(x.shape, x.dtype),
        ),
        args,
        "project",
        scratch=[pltpu.VMEM((rows, features), BF16)]
        + [pltpu.VMEM(value.shape, value.dtype) for value in args[1:]]
        + [pltpu.SemaphoreType.DMA((len(args),))],
        pin=pltpu.HBM,
        flops=2 * rows * features * width,
    )


def spread(value, count):
    def body(src, dst):
        for i in range(count):
            dst[i] = src[...]

    return local(body, pltpu.VMEM((count,) + value.shape, value.dtype), (value,), "spread")


def streams(sent, got, ties=()):
    mid = got.shape[0] // 2

    def body(first_ref, second_ref, got_ref, first_out, second_out):
        for i, (src, dst) in enumerate(((first_ref, first_out), (second_ref, second_out))):
            dst[:mid, :] = add_bf16(src[:mid, :], got_ref[i * mid : (i + 1) * mid, :])
            dst[mid:, :] = src[mid:, :]

    return local(body, tuple(shape(*v.shape) for v in sent), tuple(sent) + (got,), "streams", ties=ties)


def merge(sent, got, sums, ties=()):
    width = sent[0].shape[1]
    rows = [value.shape[0] for value in sent]

    def body(*refs):
        count = len(sums)
        for i in range(count):
            sent_ref, got_ref, out_ref = refs[i], refs[count + i], refs[2 * count + i]
            out_ref[: sums[i], :] = add_bf16(sent_ref[: sums[i], :], got_ref[: sums[i], :])
            out_ref[sums[i] : rows[i], :] = sent_ref[sums[i] :, :]
            out_ref[rows[i] :, :] = got_ref[sums[i] :, :]

    return local(
        body,
        tuple(shape(2 * r - s, width) for r, s in zip(rows, sums)),
        tuple(sent) + tuple(got),
        "merge",
        ties=ties,
    )


def settle(sent, got, orders, tok, experts, ties=()):
    width = sent[0].shape[1]
    chips = len(orders[0])
    half = chips * tok
    mid, rows = half // 2, tok // 2

    def body(first_ref, second_ref, first_got, second_got, out_ref):
        chip = lax.axis_index("expert") // 2
        out_ref[:mid, :] = add_bf16(first_ref[:mid, :], first_got[:mid, :])
        out_ref[mid:half, :] = add_bf16(second_ref[:mid, :], second_got[:mid, :])
        table = pl.ds(mid, experts)
        out_ref[pl.ds(2 * half, experts), :] = add_bf16(first_ref[table, :], first_got[table, :])
        refs = ((first_ref, first_got, mid + experts), (second_ref, second_got, mid))
        for side, (own, partner, start) in enumerate(refs):
            for place, mask in enumerate(orders[side]):
                src = own if place < chips // 2 else partner
                offset = start + (place % (chips // 2)) * rows
                to = half + pl.multiple_of((chip ^ (mask // 2)) * tok, tok) + side * rows
                out_ref[pl.ds(pl.multiple_of(to, rows), rows), :] = src[pl.ds(offset, rows), :]

    return local(body, shape(2 * half + experts, width), tuple(sent) + tuple(got), "settle", ties=ties)


def preacts(latent, up_weight, rows):
    local_experts, width, hidden = up_weight.shape

    def body(latent_ref, up, out_ref):
        for i in range(local_experts):
            out_ref[:, pl.ds(i * hidden, hidden)] = jnp.maximum(mxu(latent_ref[:rows, :], up[i]), 0.0)

    return local(
        body,
        shape(rows, local_experts * hidden, F32),
        (latent, up_weight),
        "preacts",
        limit=16,
        flops=2 * rows * width * hidden * local_experts,
    )


def experts(positive, mine, other, up_weight, down_weight):
    local_experts, width, hidden = up_weight.shape
    half = positive.shape[0]
    rows = 2 * half

    def body(positive_ref, mine_ref, other_ref, up, down, act_ref, lat_mine_ref, lat_other_ref, cot):
        me = lax.axis_index("expert")
        all_experts = mine_ref.shape[0] - rows
        ids = lax.broadcasted_iota(jnp.int32, (all_experts, 128), 0)
        slots = lax.broadcasted_iota(jnp.int32, (all_experts, 128), 1)
        pick = jnp.where(ids == slots + me * local_experts, 1.0, 0.0).astype(BF16)
        probs = []
        for src, place in ((mine_ref, 0), (other_ref, half)):
            cot[pl.ds(place, half), :] = src[half:rows, :]
            probs.append(mxu(src[rows:, :half], pick, TN))
        probs = jnp.concatenate(probs, axis=0)
        total = None
        for i in range(local_experts):
            columns = pl.ds(i * hidden, hidden)
            other = jnp.maximum(mxu(other_ref[:half, :], up[i]), 0.0)
            positive = jnp.concatenate([positive_ref[:, columns], other], axis=0)
            weighted = positive * probs[:, i : i + 1]
            act_ref[:, columns] = (positive * weighted).astype(BF16)
            grad_act = mxu(cot[...], down[i], NT)
            grad_pre = (grad_act * (2.0 * weighted)).astype(BF16)
            term = mxu(grad_pre, up[i], NT)
            total = term if total is None else total + term
        lat_mine_ref[...] = total[:half].astype(BF16)
        lat_other_ref[...] = total[half:].astype(BF16)

    return local(
        body,
        (shape(rows, local_experts * hidden), shape(half, width), shape(half, width)),
        (positive, mine, other, up_weight, down_weight),
        "experts",
        scratch=[pltpu.VMEM((rows, width), BF16)],
        limit=24,
        flops=2 * 5 * half * width * hidden * local_experts,
    )


def outputs(act, down_weight, half):
    local_experts, hidden, width = down_weight.shape

    def body(act_ref, down, mine_ref, other_ref):
        total = None
        for i in range(local_experts):
            term = mxu(act_ref[:, pl.ds(i * hidden, hidden)], down[i])
            total = term if total is None else total + term
        mine_ref[...] = total[:half].astype(BF16)
        other_ref[...] = total[half:].astype(BF16)

    return local(
        body,
        (shape(half, width), shape(half, width)),
        (act, down_weight),
        "outputs",
        limit=16,
        flops=4 * half * local_experts * hidden * width,
    )


def pieces_of(first, second, chips, ties=()):
    rows, width = first.shape
    tok = rows // chips

    def body(first_ref, second_ref, *out_refs):
        chip = lax.axis_index("expert") // 2
        for mask in range(chips):
            rows = block(chip ^ mask, tok)
            out_refs[mask][...] = add_bf16(first_ref[rows, :], second_ref[rows, :])

    return local(body, tuple(shape(tok, width) for _ in range(chips)), (first, second), "pieces", ties=ties)


def scatter(pieces):
    return [xor_permute(pieces[k], "expert", 2 * k) for k in range(1, len(pieces))]


def add_pieces(pieces, start=0, ties=()):
    rows, width = pieces[0].shape

    def body(*refs):
        total = refs[0][...].astype(F32)
        for ref in refs[1:-1]:
            total = total + ref[pl.ds(start, rows), :].astype(F32)
        refs[-1][...] = total.astype(BF16)

    return local(body, shape(rows, width), tuple(pieces), "add_pieces", ties=ties)


def head(value, tails, ties=()):
    rows, width = value.shape
    count = len(tails)

    def body(*refs):
        for tail, out in zip(refs[1 : 1 + count], refs[1 + count :]):
            out[pl.ds(0, rows), :] = refs[0][...]
            out[pl.ds(rows, tail.shape[0]), :] = tail[...]

    outs = tuple(shape(rows + tail.shape[0], width) for tail in tails)
    return local(body, outs, (value, *tails), "head", ties=ties)


def stack(values, rows, ties=(), flops=0):
    width = values[0].shape[1]

    def body(*refs):
        for i, ref in enumerate(refs[:-1]):
            refs[-1][pl.ds(i * rows, rows), :] = ref[pl.ds(0, rows), :]

    return local(body, shape(len(values) * rows, width), tuple(values), "stack", ties=ties, flops=flops)


def input_grads(near, twins, in_proj, tok):
    features, width = in_proj.shape
    rows = 2 * near.shape[0]

    def body(near_ref, twins_ref, proj_ref, out_ref, rows_ref):
        me = lax.axis_index("expert")
        for mask in range(rows // tok):
            src = (near_ref, twins_ref)[mask % 2]
            rows_ref[block(me ^ mask, tok), :] = src[pl.ds(mask // 2 * tok, tok), :]
        out_ref[...] = mxu(rows_ref[...], proj_ref[...], NT).astype(BF16)

    return local(
        body,
        shape(rows, features),
        (near, twins, in_proj),
        "input_grads",
        scratch=[pltpu.VMEM((rows, width), BF16)],
        limit=16,
        flops=2 * rows * features * width,
    )


def arrange(value, chips, tok, tie):
    count, rows, features = value.shape

    def body(x_ref, *out_refs):
        me = lax.axis_index("expert")
        group = lax.axis_index("dp") if count > 1 else 0
        for mask in range(count):
            for k in range(chips):
                for twin in range(2):
                    out_refs[k][pl.ds((twin * count + mask) * tok, tok), :] = x_ref[
                        group ^ mask, block(me ^ (2 * k + twin), tok), :
                    ]

    out = tuple(shape(2 * count * tok, features) for _ in range(chips))
    return local(body, out, (value,), "arrange", ties=(tie,))


def proj_round(x_rows, near, far, chip, tok, before, last):
    rows, features = x_rows.shape
    width = near[0].shape[1]
    given = [x_rows, *near, *far] + ([] if before is None else [before])
    steps = 4 if features % 512 == 0 else 1
    tile = features // steps

    def body(*refs):
        x_ref = refs[0]
        out_ref, rows_ref = refs[len(given)], refs[len(given) + 1]
        for twin in range(2):
            start = twin * (rows // 2)
            rows_ref[pl.ds(start, tok), :] = refs[1 + twin][pl.ds(chip * tok, tok), :]
            if far:
                rows_ref[pl.ds(start + tok, rows // 2 - tok), :] = refs[3 + twin][...]
        copies = []
        for i in range(steps):
            part = pl.ds(i * tile, tile)
            total = mxu(x_ref[:, part], rows_ref[...], TN)
            if before is not None:
                total = total + refs[len(given) - 1][part, :]
            if last:
                whole_ref, sems = refs[len(given) + 2], refs[len(given) + 3]
                whole_ref[part, :] = total
                copies.append(pltpu.make_async_copy(whole_ref.at[part], out_ref.at[part], sems.at[i]))
                copies[-1].start()
            else:
                out_ref[part, :] = total
        for copy in copies:
            copy.wait()

    scratch = [pltpu.VMEM((rows, width), BF16)]
    if last:
        scratch += [pltpu.VMEM((features, width), F32), pltpu.SemaphoreType.DMA((steps,))]
    return pl.pallas_call(
        body,
        out_shape=shape(features, width, F32),
        in_specs=[VMEM] * len(given),
        out_specs=ANY if last else VMEM,
        scratch_shapes=scratch,
        compiler_params=pltpu.CompilerParams(vmem_limit_bytes=16 * MIB),
        cost_estimate=pl.CostEstimate(
            flops=2 * rows * features * width, bytes_accessed=4 * MIB, transcendentals=0
        ),
        name="proj_round",
    )(*given)


def per_device(tokens_x, in_proj, up_weight, down_weight, expert_ids, route_probs, out_grad):
    owners = lax.axis_size("expert")
    groups = lax.axis_size("dp")
    chips = owners // 2
    chip = lax.axis_index("expert") // 2
    tok, top = expert_ids.shape
    all_experts = up_weight.shape[0] * owners
    features, width = in_proj.shape
    half = chips * tok
    bits = [1 << b for b in range(1, owners.bit_length() - 1)]
    gather_groups = groups == 4 and groups * owners * tok * width <= 1 << 22

    part_other, *sent, x_own = project(
        tokens_x, in_proj, out_grad, expert_ids, route_probs, all_experts
    )
    sums = (half // 2 + all_experts, half // 2)
    x_groups, x_spread = x_own[None], ()
    if gather_groups:
        x_spread = spread(x_own, groups)
        x_groups = lax.all_to_all(x_spread, "dp", split_axis=0, concat_axis=0, tiled=True)
    up, down = load(up_weight, down_weight)
    sent = streams(sent, xor_permute(part_other, "expert", 1), (x_spread,) if gather_groups else ())
    for step, stream_bits in enumerate(zip(bits, bits[::-1])):
        got = [xor_permute(value, "expert", bit) for value, bit in zip(sent, stream_bits)]
        if step + 1 < len(bits):
            sent = merge(sent, got, sums)
    mine = settle(sent, got, (order_of(bits), order_of(bits[::-1])), tok, all_experts, ties=(up, down))
    other = xor_permute(mine, "expert", 1)

    positive = preacts(mine, up, half)
    act, lat_mine, lat_other = experts(positive, mine, other, up, down)
    out_mine, out_other = outputs(act, down, half)
    out_pieces = pieces_of(out_mine, xor_permute(out_other, "expert", 1), chips)
    lat_pieces = pieces_of(lat_mine, xor_permute(lat_other, "expert", 1), chips)
    got = scatter(lat_pieces)
    latent_grad = add_pieces((lat_pieces[0], *got))

    own = ()
    if gather_groups:
        across = [xor_permute(latent_grad, "dp", m) for m in range(1, groups)]
        own = stack(across, tok, ties=(x_groups,))
    after = (own,) if gather_groups else ()
    sent = head(latent_grad, out_pieces[1:])
    got = scatter([None, *sent])
    combined = add_pieces((out_pieces[0], *got), tok, ties=after)
    near = stack([latent_grad, *got], tok, ties=after)
    parts = 2
    split = near.shape[0] // parts
    twins = [xor_permute(near[i * split : (i + 1) * split], "expert", 1) for i in range(parts)]
    twins = jnp.concatenate(twins, axis=0)
    input_grad = input_grads(near, twins, in_proj, tok)
    far = [() for _ in range(chips)]
    x_all = arrange(x_groups, chips, tok, latent_grad)
    order = [0] + list(range(chips - 1, 0, -1))
    if gather_groups:
        far[0] = (own, xor_permute(own, "expert", 1))
    proj_grad = proj_round(x_all[0], (near, twins), far[0], 0, tok, None, False)
    if gather_groups:
        pieces = {k: xor_permute(own, "expert", 2 * k) for k in order[1:]}
        for k in order[1:]:
            if k == order[-1]:
                ties = (proj_grad, input_grad, combined)
            else:
                ties = (pieces[order[-1]],) if k == order[-2] else ()
            relay = stack([pieces[k]], pieces[k].shape[0], ties)
            far[k] = (relay, xor_permute(relay, "expert", 1))
    for k in order[1:]:
        proj_grad = proj_round(x_all[k], (near, twins), far[k], k, tok, proj_grad, k == order[-1])
    if not gather_groups:
        proj_grad = lax.psum(proj_grad, "dp")
    return (combined, input_grad, proj_grad)


def solution(mesh):
    return jax.shard_map(
        per_device,
        mesh=mesh,
        in_specs=(
            P("dp", "expert"),
            P("expert", None),
            P("expert", None, None),
            P("expert", None, None),
            P(("dp", "expert"), None),
            P(("dp", "expert"), None),
            P(("dp", "expert"), None),
        ),
        out_specs=(P(("dp", "expert"), None), P("dp", "expert"), P("expert", None)),
        check_vma=False,
    )
```

```python
import jax
import jax.numpy as jnp
from jax import lax
from jax.experimental import pallas as pl
from jax.experimental.pallas import tpu as pltpu
from jax.sharding import PartitionSpec as P

VMEM = pl.BlockSpec(memory_space=pltpu.VMEM)
ANY = pl.BlockSpec(memory_space=pl.ANY)
BF16 = jnp.bfloat16
F32 = jnp.float32
NN = (((1,), (0,)), ((), ()))
NT = (((1,), (1,)), ((), ()))
TN = (((0,), (0,)), ((), ()))
MIB = 1 << 20
STEPS = 4


def mxu(first, second, dims=NN):
    return lax.dot_general(first, second, dims, preferred_element_type=F32)


def shape(rows, columns, dtype=BF16):
    return jax.ShapeDtypeStruct((rows, columns), dtype)


def add_bf16(first, second):
    return (first.astype(F32) + second.astype(F32)).astype(BF16)


def local(body, outs, args, name, scratch=(), limit=8, flops=0, ties=(), pin=None):
    single = not isinstance(outs, tuple)
    spec = VMEM if pin is None else pl.BlockSpec(memory_space=pin)

    def kernel(*refs):
        body(*refs[: len(args)], *refs[len(args) + len(ties) :])

    if pin is not None:
        args = [pltpu.with_memory_space_constraint(value, pin) for value in args]
    return pl.pallas_call(
        kernel,
        out_shape=outs,
        in_specs=[spec] * len(args) + [ANY] * len(ties),
        out_specs=VMEM if single else tuple(VMEM for _ in outs),
        scratch_shapes=list(scratch),
        compiler_params=pltpu.CompilerParams(vmem_limit_bytes=limit * MIB),
        cost_estimate=pl.CostEstimate(flops=flops, bytes_accessed=MIB, transcendentals=0),
        name=name,
    )(*args, *ties)


def load(*values):
    count = len(values)
    parts = [(j, i) for i in range(values[0].shape[0]) for j in range(count)]

    def body(*refs):
        copies = [
            pltpu.make_async_copy(refs[j].at[i], refs[count + j].at[i], refs[2 * count].at[place])
            for place, (j, i) in enumerate(parts)
        ]
        for copy in copies:
            copy.start()
        for copy in copies:
            copy.wait()

    return local(
        body,
        tuple(pltpu.VMEM(value.shape, value.dtype) for value in values),
        values,
        "load",
        scratch=[pltpu.SemaphoreType.DMA((len(parts),))],
        pin=pltpu.HBM,
    )


def xor_permute(value, axis, mask):
    size = lax.axis_size(axis)
    return lax.ppermute(value, axis, [(i, i ^ mask) for i in range(size)])


def order_of(bits):
    masks = [0]
    for bit in bits:
        masks = masks + [mask ^ bit for mask in masks]
    return masks


def block(index, rows):
    return pl.ds(pl.multiple_of(index * rows, rows), rows)


def project(x, in_proj, out_grad, expert_ids, route_probs, all_experts):
    rows, features = x.shape
    width = in_proj.shape[1]
    tok, top = out_grad.shape[0], expert_ids.shape[1]
    chips = rows // tok // 2
    half, mid, cot = rows // 2, rows // 4, tok // 2

    args = (x, in_proj, out_grad, expert_ids.T, route_probs.T)

    def body(*refs):
        other_ref, first_ref, second_ref, x_ref, rows_ref = refs[5:10]
        proj_ref, grad_ref, ids_ref, probs_ref = refs[10:14]
        held = (x_ref, proj_ref, grad_ref, ids_ref, probs_ref)
        copies = [
            pltpu.make_async_copy(refs[i], held[i], refs[14].at[i]) for i in range(len(args))
        ]
        for copy in copies:
            copy.start()
        copies[0].wait()
        me = lax.axis_index("expert")
        core = me % 2
        for chip in range(chips):
            rows_ref[pl.ds(chip * tok, tok), :] = x_ref[block(2 * chip + 1 - core, tok), :]
            rows_ref[pl.ds(half + chip * tok, tok), :] = x_ref[block(2 * chip + core, tok), :]
        copies[1].wait()
        other_ref[...] = mxu(rows_ref[:half, :], proj_ref[...]).astype(BF16)
        mine = mxu(rows_ref[half:, :], proj_ref[...]).astype(BF16)
        first_ref[:mid, :] = mine[:mid]
        second_ref[:mid, :] = mine[mid:]
        for copy in copies[2:]:
            copy.wait()
        names = lax.broadcasted_iota(jnp.int32, (all_experts, tok), 0)
        table = jnp.zeros((all_experts, tok), F32)
        for k in range(top):
            table += jnp.where(names == ids_ref[k : k + 1, :], probs_ref[k : k + 1, :], 0.0)
        token = lax.broadcasted_iota(jnp.int32, (tok, width), 0)
        column = lax.broadcasted_iota(jnp.int32, (tok, width), 1)
        place = jnp.where(column == token + (me // 2) * tok, 1.0, 0.0).astype(BF16)
        first_ref[mid : mid + all_experts, :] = mxu(table.astype(BF16), place).astype(BF16)
        first_ref[mid + all_experts :, :] = grad_ref[:cot, :]
        second_ref[mid:, :] = grad_ref[cot:, :]

    return local(
        body,
        (
            shape(half, width),
            shape(mid + all_experts + cot, width),
            shape(mid + cot, width),
            pltpu.VMEM(x.shape, x.dtype),
        ),
        args,
        "project",
        scratch=[pltpu.VMEM((rows, features), BF16)]
        + [pltpu.VMEM(value.shape, value.dtype) for value in args[1:]]
        + [pltpu.SemaphoreType.DMA((len(args),))],
        pin=pltpu.HBM,
        flops=2 * rows * features * width,
    )


def spread(value, count):
    def body(src, dst):
        for i in range(count):
            dst[i] = src[...]

    return local(body, pltpu.VMEM((count,) + value.shape, value.dtype), (value,), "spread")


def streams(sent, got, ties=()):
    mid = got.shape[0] // 2

    def body(first_ref, second_ref, got_ref, first_out, second_out):
        for i, (src, dst) in enumerate(((first_ref, first_out), (second_ref, second_out))):
            dst[:mid, :] = add_bf16(src[:mid, :], got_ref[i * mid : (i + 1) * mid, :])
            dst[mid:, :] = src[mid:, :]

    return local(body, tuple(shape(*v.shape) for v in sent), tuple(sent) + (got,), "streams", ties=ties)


def merge(sent, got, sums, ties=()):
    width = sent[0].shape[1]
    rows = [value.shape[0] for value in sent]

    def body(*refs):
        count = len(sums)
        for i in range(count):
            sent_ref, got_ref, out_ref = refs[i], refs[count + i], refs[2 * count + i]
            out_ref[: sums[i], :] = add_bf16(sent_ref[: sums[i], :], got_ref[: sums[i], :])
            out_ref[sums[i] : rows[i], :] = sent_ref[sums[i] :, :]
            out_ref[rows[i] :, :] = got_ref[sums[i] :, :]

    return local(
        body,
        tuple(shape(2 * r - s, width) for r, s in zip(rows, sums)),
        tuple(sent) + tuple(got),
        "merge",
        ties=ties,
    )


def settle(sent, got, orders, tok, experts, ties=()):
    width = sent[0].shape[1]
    chips = len(orders[0])
    half = chips * tok
    mid, rows = half // 2, tok // 2

    def body(first_ref, second_ref, first_got, second_got, out_ref):
        chip = lax.axis_index("expert") // 2
        out_ref[:mid, :] = add_bf16(first_ref[:mid, :], first_got[:mid, :])
        out_ref[mid:half, :] = add_bf16(second_ref[:mid, :], second_got[:mid, :])
        table = pl.ds(mid, experts)
        out_ref[pl.ds(2 * half, experts), :] = add_bf16(first_ref[table, :], first_got[table, :])
        refs = ((first_ref, first_got, mid + experts), (second_ref, second_got, mid))
        for side, (own, partner, start) in enumerate(refs):
            for place, mask in enumerate(orders[side]):
                src = own if place < chips // 2 else partner
                offset = start + (place % (chips // 2)) * rows
                to = half + pl.multiple_of((chip ^ (mask // 2)) * tok, tok) + side * rows
                out_ref[pl.ds(pl.multiple_of(to, rows), rows), :] = src[pl.ds(offset, rows), :]

    return local(body, shape(2 * half + experts, width), tuple(sent) + tuple(got), "settle", ties=ties)


def preacts(latent, up_weight, rows):
    local_experts, width, hidden = up_weight.shape

    def body(latent_ref, up, out_ref):
        for i in range(local_experts):
            out_ref[:, pl.ds(i * hidden, hidden)] = jnp.maximum(mxu(latent_ref[:rows, :], up[i]), 0.0)

    return local(
        body,
        shape(rows, local_experts * hidden, F32),
        (latent, up_weight),
        "preacts",
        limit=16,
        flops=2 * rows * width * hidden * local_experts,
    )


def experts(positive, mine, other, up_weight, down_weight):
    local_experts, width, hidden = up_weight.shape
    half = positive.shape[0]
    rows = 2 * half

    def body(positive_ref, mine_ref, other_ref, up, down, act_ref, lat_mine_ref, lat_other_ref, cot):
        me = lax.axis_index("expert")
        all_experts = mine_ref.shape[0] - rows
        ids = lax.broadcasted_iota(jnp.int32, (all_experts, 128), 0)
        slots = lax.broadcasted_iota(jnp.int32, (all_experts, 128), 1)
        pick = jnp.where(ids == slots + me * local_experts, 1.0, 0.0).astype(BF16)
        probs = []
        for src, place in ((mine_ref, 0), (other_ref, half)):
            cot[pl.ds(place, half), :] = src[half:rows, :]
            probs.append(mxu(src[rows:, :half], pick, TN))
        probs = jnp.concatenate(probs, axis=0)
        total = None
        for i in range(local_experts):
            columns = pl.ds(i * hidden, hidden)
            other = jnp.maximum(mxu(other_ref[:half, :], up[i]), 0.0)
            positive = jnp.concatenate([positive_ref[:, columns], other], axis=0)
            weighted = positive * probs[:, i : i + 1]
            act_ref[:, columns] = (positive * weighted).astype(BF16)
            grad_act = mxu(cot[...], down[i], NT)
            grad_pre = (grad_act * (2.0 * weighted)).astype(BF16)
            term = mxu(grad_pre, up[i], NT)
            total = term if total is None else total + term
        lat_mine_ref[...] = total[:half].astype(BF16)
        lat_other_ref[...] = total[half:].astype(BF16)

    return local(
        body,
        (shape(rows, local_experts * hidden), shape(half, width), shape(half, width)),
        (positive, mine, other, up_weight, down_weight),
        "experts",
        scratch=[pltpu.VMEM((rows, width), BF16)],
        limit=24,
        flops=2 * 5 * half * width * hidden * local_experts,
    )


def outputs(act, down_weight, half):
    local_experts, hidden, width = down_weight.shape

    def body(act_ref, down, mine_ref, other_ref):
        total = None
        for i in range(local_experts):
            term = mxu(act_ref[:, pl.ds(i * hidden, hidden)], down[i])
            total = term if total is None else total + term
        mine_ref[...] = total[:half].astype(BF16)
        other_ref[...] = total[half:].astype(BF16)

    return local(
        body,
        (shape(half, width), shape(half, width)),
        (act, down_weight),
        "outputs",
        limit=16,
        flops=4 * half * local_experts * hidden * width,
    )


def pieces_of(first, second, chips, ties=()):
    rows, width = first.shape
    tok = rows // chips

    def body(first_ref, second_ref, *out_refs):
        chip = lax.axis_index("expert") // 2
        for mask in range(chips):
            rows = block(chip ^ mask, tok)
            out_refs[mask][...] = add_bf16(first_ref[rows, :], second_ref[rows, :])

    return local(body, tuple(shape(tok, width) for _ in range(chips)), (first, second), "pieces", ties=ties)


def scatter(pieces):
    return [xor_permute(pieces[k], "expert", 2 * k) for k in range(1, len(pieces))]


def add_pieces(pieces, start=0, ties=()):
    rows, width = pieces[0].shape

    def body(*refs):
        total = refs[0][...].astype(F32)
        for ref in refs[1:-1]:
            total = total + ref[pl.ds(start, rows), :].astype(F32)
        refs[-1][...] = total.astype(BF16)

    return local(body, shape(rows, width), tuple(pieces), "add_pieces", ties=ties)


def head(value, tails, ties=()):
    rows, width = value.shape
    count = len(tails)

    def body(*refs):
        for tail, out in zip(refs[1 : 1 + count], refs[1 + count :]):
            out[pl.ds(0, rows), :] = refs[0][...]
            out[pl.ds(rows, tail.shape[0]), :] = tail[...]

    outs = tuple(shape(rows + tail.shape[0], width) for tail in tails)
    return local(body, outs, (value, *tails), "head", ties=ties)


def stack(values, rows, ties=(), flops=0):
    width = values[0].shape[1]

    def body(*refs):
        for i, ref in enumerate(refs[:-1]):
            refs[-1][pl.ds(i * rows, rows), :] = ref[pl.ds(0, rows), :]

    return local(body, shape(len(values) * rows, width), tuple(values), "stack", ties=ties, flops=flops)


def arrange(value, chips, tok, tie):
    count, rows, features = value.shape

    def body(x_ref, out_ref):
        me = lax.axis_index("expert")
        group = lax.axis_index("dp") if count > 1 else 0
        for side in range(2 * chips):
            for mask in range(count):
                out_ref[pl.ds((side * count + mask) * tok, tok), :] = x_ref[
                    group ^ mask, block(me ^ side, tok), :
                ]

    return local(body, shape(count * rows, features), (value,), "arrange", ties=(tie,))


def finish(x_rows, near, twins, far, in_proj, tok):
    rows, features = x_rows.shape
    width = near.shape[1]
    sides = 2 * near.shape[0] // tok
    count = rows // tok // sides
    far = [piece for pair in far for piece in pair]
    given = (x_rows, near, twins, in_proj, *far)
    steps = STEPS if features % (128 * STEPS) == 0 else 1
    tile = features // steps

    def body(*refs):
        x_ref, near_ref, twins_ref, in_proj_ref = refs[:4]
        far_refs = refs[4 : len(given)]
        input_ref, proj_ref, rows_ref, whole_ref, own_ref, result_ref, sems = refs[len(given) :]
        me = lax.axis_index("expert")
        for side in range(sides):
            src = (near_ref, twins_ref)[side % 2]
            piece = src[pl.ds(side // 2 * tok, tok), :]
            rows_ref[pl.ds(side * count * tok, tok), :] = piece
            own_ref[block(me ^ side, tok), :] = piece
            if far_refs:
                rows_ref[pl.ds((side * count + 1) * tok, (count - 1) * tok), :] = far_refs[side][...]
        copies = []
        for i in range(steps):
            part = pl.ds(i * tile, tile)
            whole_ref[part, :] = mxu(x_ref[:, part], rows_ref[...], TN)
            copies.append(pltpu.make_async_copy(whole_ref.at[part], proj_ref.at[part], sems.at[i]))
            copies[-1].start()
        result_ref[...] = mxu(own_ref[...], in_proj_ref[...], NT).astype(BF16)
        copies.append(pltpu.make_async_copy(result_ref, input_ref, sems.at[steps]))
        copies[-1].start()
        for copy in copies:
            copy.wait()

    own_rows = sides * tok
    return pl.pallas_call(
        body,
        out_shape=(shape(own_rows, features), shape(features, width, F32)),
        in_specs=[VMEM] * len(given),
        out_specs=(ANY, ANY),
        scratch_shapes=[
            pltpu.VMEM((rows, width), BF16),
            pltpu.VMEM((features, width), F32),
            pltpu.VMEM((own_rows, width), BF16),
            pltpu.VMEM((own_rows, features), BF16),
            pltpu.SemaphoreType.DMA((steps + 1,)),
        ],
        compiler_params=pltpu.CompilerParams(vmem_limit_bytes=24 * MIB),
        cost_estimate=pl.CostEstimate(
            flops=2 * rows * features * width, bytes_accessed=4 * MIB, transcendentals=0
        ),
        name="finish",
    )(*given)


def per_device(tokens_x, in_proj, up_weight, down_weight, expert_ids, route_probs, out_grad):
    owners = lax.axis_size("expert")
    groups = lax.axis_size("dp")
    chips = owners // 2
    chip = lax.axis_index("expert") // 2
    tok, top = expert_ids.shape
    all_experts = up_weight.shape[0] * owners
    features, width = in_proj.shape
    half = chips * tok
    bits = [1 << b for b in range(1, owners.bit_length() - 1)]
    gather_groups = groups == 4 and groups * owners * tok * width <= 1 << 22

    part_other, *sent, x_own = project(
        tokens_x, in_proj, out_grad, expert_ids, route_probs, all_experts
    )
    sums = (half // 2 + all_experts, half // 2)
    x_groups, x_spread = x_own[None], ()
    if gather_groups:
        x_spread = spread(x_own, groups)
        x_groups = lax.all_to_all(x_spread, "dp", split_axis=0, concat_axis=0, tiled=True)
    up, down = load(up_weight, down_weight)
    sent = streams(sent, xor_permute(part_other, "expert", 1), (x_spread,) if gather_groups else ())
    for step, stream_bits in enumerate(zip(bits, bits[::-1])):
        got = [xor_permute(value, "expert", bit) for value, bit in zip(sent, stream_bits)]
        if step + 1 < len(bits):
            sent = merge(sent, got, sums)
    mine = settle(sent, got, (order_of(bits), order_of(bits[::-1])), tok, all_experts, ties=(up, down))
    other = xor_permute(mine, "expert", 1)

    positive = preacts(mine, up, half)
    act, lat_mine, lat_other = experts(positive, mine, other, up, down)
    out_mine, out_other = outputs(act, down, half)
    out_pieces = pieces_of(out_mine, xor_permute(out_other, "expert", 1), chips)
    lat_pieces = pieces_of(lat_mine, xor_permute(lat_other, "expert", 1), chips)
    got = scatter(lat_pieces)
    latent_grad = add_pieces((lat_pieces[0], *got))

    own = ()
    if gather_groups:
        across = [xor_permute(latent_grad, "dp", m) for m in range(1, groups)]
        own = stack(across, tok, ties=(x_groups,))
    after = (own,) if gather_groups else ()
    sent = head(latent_grad, out_pieces[1:])
    got = scatter([None, *sent])
    combined = add_pieces((out_pieces[0], *got), tok, ties=after)
    near = stack([latent_grad, *got], tok, ties=after)
    parts = 2
    split = near.shape[0] // parts
    twins = [xor_permute(near[i * split : (i + 1) * split], "expert", 1) for i in range(parts)]
    twins = jnp.concatenate(twins, axis=0)
    x_rows = arrange(x_groups, chips, tok, latent_grad)
    far = []
    if gather_groups:
        pieces = [own] + [xor_permute(own, "expert", 2 * k) for k in range(1, chips)]
        far = [(piece, xor_permute(piece, "expert", 1)) for piece in pieces]
    input_grad, proj_grad = finish(x_rows, near, twins, far, in_proj, tok)
    if not gather_groups:
        proj_grad = lax.psum(proj_grad, "dp")
    return (combined, input_grad, proj_grad)


def solution(mesh):
    return jax.shard_map(
        per_device,
        mesh=mesh,
        in_specs=(
            P("dp", "expert"),
            P("expert", None),
            P("expert", None, None),
            P("expert", None, None),
            P(("dp", "expert"), None),
            P(("dp", "expert"), None),
            P(("dp", "expert"), None),
        ),
        out_specs=(P(("dp", "expert"), None), P("dp", "expert"), P("expert", None)),
        check_vma=False,
    )
```

```python
import jax
import jax.numpy as jnp
from jax import lax
from jax.experimental import pallas as pl
from jax.experimental.pallas import tpu as pltpu
from jax.sharding import PartitionSpec as P

VMEM = pl.BlockSpec(memory_space=pltpu.VMEM)
ANY = pl.BlockSpec(memory_space=pl.ANY)
BF16 = jnp.bfloat16
F32 = jnp.float32
NN = (((1,), (0,)), ((), ()))
NT = (((1,), (1,)), ((), ()))
TN = (((0,), (0,)), ((), ()))
MIB = 1 << 20
STEPS = 4


def mxu(first, second, dims=NN):
    return lax.dot_general(first, second, dims, preferred_element_type=F32)


def shape(rows, columns, dtype=BF16):
    return jax.ShapeDtypeStruct((rows, columns), dtype)


def add_bf16(first, second):
    return (first.astype(F32) + second.astype(F32)).astype(BF16)


def local(body, outs, args, name, scratch=(), limit=8, flops=0, ties=(), pin=None):
    single = not isinstance(outs, tuple)
    spec = VMEM if pin is None else pl.BlockSpec(memory_space=pin)

    def kernel(*refs):
        body(*refs[: len(args)], *refs[len(args) + len(ties) :])

    if pin is not None:
        args = [pltpu.with_memory_space_constraint(value, pin) for value in args]
    return pl.pallas_call(
        kernel,
        out_shape=outs,
        in_specs=[spec] * len(args) + [ANY] * len(ties),
        out_specs=VMEM if single else tuple(VMEM for _ in outs),
        scratch_shapes=list(scratch),
        compiler_params=pltpu.CompilerParams(vmem_limit_bytes=limit * MIB),
        cost_estimate=pl.CostEstimate(flops=flops, bytes_accessed=MIB, transcendentals=0),
        name=name,
    )(*args, *ties)


def load(*values):
    count = len(values)
    parts = [(j, i) for i in range(values[0].shape[0]) for j in range(count)]

    def body(*refs):
        copies = [
            pltpu.make_async_copy(refs[j].at[i], refs[count + j].at[i], refs[2 * count].at[place])
            for place, (j, i) in enumerate(parts)
        ]
        for copy in copies:
            copy.start()
        for copy in copies:
            copy.wait()

    return local(
        body,
        tuple(pltpu.VMEM(value.shape, value.dtype) for value in values),
        values,
        "load",
        scratch=[pltpu.SemaphoreType.DMA((len(parts),))],
        pin=pltpu.HBM,
    )


def xor_permute(value, axis, mask):
    size = lax.axis_size(axis)
    return lax.ppermute(value, axis, [(i, i ^ mask) for i in range(size)])


def order_of(bits):
    masks = [0]
    for bit in bits:
        masks = masks + [mask ^ bit for mask in masks]
    return masks


def block(index, rows):
    return pl.ds(pl.multiple_of(index * rows, rows), rows)


def project(x, in_proj, out_grad, expert_ids, route_probs, all_experts):
    rows, features = x.shape
    width = in_proj.shape[1]
    tok, top = out_grad.shape[0], expert_ids.shape[1]
    chips = rows // tok // 2
    half, mid, cot = rows // 2, rows // 4, tok // 2

    args = (x, in_proj, out_grad, expert_ids.T, route_probs.T)

    def body(*refs):
        other_ref, first_ref, second_ref, x_ref, rows_ref = refs[5:10]
        proj_ref, grad_ref, ids_ref, probs_ref = refs[10:14]
        held = (x_ref, proj_ref, grad_ref, ids_ref, probs_ref)
        copies = [
            pltpu.make_async_copy(refs[i], held[i], refs[14].at[i]) for i in range(len(args))
        ]
        for copy in copies:
            copy.start()
        copies[0].wait()
        me = lax.axis_index("expert")
        core = me % 2
        for chip in range(chips):
            rows_ref[pl.ds(chip * tok, tok), :] = x_ref[block(2 * chip + 1 - core, tok), :]
            rows_ref[pl.ds(half + chip * tok, tok), :] = x_ref[block(2 * chip + core, tok), :]
        copies[1].wait()
        other_ref[...] = mxu(rows_ref[:half, :], proj_ref[...]).astype(BF16)
        mine = mxu(rows_ref[half:, :], proj_ref[...]).astype(BF16)
        first_ref[:mid, :] = mine[:mid]
        second_ref[:mid, :] = mine[mid:]
        for copy in copies[2:]:
            copy.wait()
        names = lax.broadcasted_iota(jnp.int32, (all_experts, tok), 0)
        table = jnp.zeros((all_experts, tok), F32)
        for k in range(top):
            table += jnp.where(names == ids_ref[k : k + 1, :], probs_ref[k : k + 1, :], 0.0)
        token = lax.broadcasted_iota(jnp.int32, (tok, width), 0)
        column = lax.broadcasted_iota(jnp.int32, (tok, width), 1)
        place = jnp.where(column == token + (me // 2) * tok, 1.0, 0.0).astype(BF16)
        first_ref[mid : mid + all_experts, :] = mxu(table.astype(BF16), place).astype(BF16)
        first_ref[mid + all_experts :, :] = grad_ref[:cot, :]
        second_ref[mid:, :] = grad_ref[cot:, :]

    return local(
        body,
        (
            shape(half, width),
            shape(mid + all_experts + cot, width),
            shape(mid + cot, width),
            pltpu.VMEM(x.shape, x.dtype),
        ),
        args,
        "project",
        scratch=[pltpu.VMEM((rows, features), BF16)]
        + [pltpu.VMEM(value.shape, value.dtype) for value in args[1:]]
        + [pltpu.SemaphoreType.DMA((len(args),))],
        pin=pltpu.HBM,
        flops=2 * rows * features * width,
    )


def spread(value, count):
    def body(src, dst):
        for i in range(count):
            dst[i] = src[...]

    return local(body, pltpu.VMEM((count,) + value.shape, value.dtype), (value,), "spread")


def streams(sent, got, ties=()):
    mid = got.shape[0] // 2

    def body(first_ref, second_ref, got_ref, first_out, second_out):
        for i, (src, dst) in enumerate(((first_ref, first_out), (second_ref, second_out))):
            dst[:mid, :] = add_bf16(src[:mid, :], got_ref[i * mid : (i + 1) * mid, :])
            dst[mid:, :] = src[mid:, :]

    return local(body, tuple(shape(*v.shape) for v in sent), tuple(sent) + (got,), "streams", ties=ties)


def merge(sent, got, sums, ties=()):
    width = sent[0].shape[1]
    rows = [value.shape[0] for value in sent]

    def body(*refs):
        count = len(sums)
        for i in range(count):
            sent_ref, got_ref, out_ref = refs[i], refs[count + i], refs[2 * count + i]
            out_ref[: sums[i], :] = add_bf16(sent_ref[: sums[i], :], got_ref[: sums[i], :])
            out_ref[sums[i] : rows[i], :] = sent_ref[sums[i] :, :]
            out_ref[rows[i] :, :] = got_ref[sums[i] :, :]

    return local(
        body,
        tuple(shape(2 * r - s, width) for r, s in zip(rows, sums)),
        tuple(sent) + tuple(got),
        "merge",
        ties=ties,
    )


def settle(sent, got, orders, tok, experts, ties=()):
    width = sent[0].shape[1]
    chips = len(orders[0])
    half = chips * tok
    mid, rows = half // 2, tok // 2

    def body(first_ref, second_ref, first_got, second_got, out_ref):
        chip = lax.axis_index("expert") // 2
        out_ref[:mid, :] = add_bf16(first_ref[:mid, :], first_got[:mid, :])
        out_ref[mid:half, :] = add_bf16(second_ref[:mid, :], second_got[:mid, :])
        table = pl.ds(mid, experts)
        out_ref[pl.ds(2 * half, experts), :] = add_bf16(first_ref[table, :], first_got[table, :])
        refs = ((first_ref, first_got, mid + experts), (second_ref, second_got, mid))
        for side, (own, partner, start) in enumerate(refs):
            for place, mask in enumerate(orders[side]):
                src = own if place < chips // 2 else partner
                offset = start + (place % (chips // 2)) * rows
                to = half + pl.multiple_of((chip ^ (mask // 2)) * tok, tok) + side * rows
                out_ref[pl.ds(pl.multiple_of(to, rows), rows), :] = src[pl.ds(offset, rows), :]

    return local(body, shape(2 * half + experts, width), tuple(sent) + tuple(got), "settle", ties=ties)


def preacts(latent, up_weight, rows):
    local_experts, width, hidden = up_weight.shape

    def body(latent_ref, up, out_ref):
        for i in range(local_experts):
            out_ref[:, pl.ds(i * hidden, hidden)] = jnp.maximum(mxu(latent_ref[:rows, :], up[i]), 0.0)

    return local(
        body,
        shape(rows, local_experts * hidden, F32),
        (latent, up_weight),
        "preacts",
        limit=16,
        flops=2 * rows * width * hidden * local_experts,
    )


def experts(positive, mine, other, up_weight, down_weight):
    local_experts, width, hidden = up_weight.shape
    half = positive.shape[0]
    rows = 2 * half

    def body(positive_ref, mine_ref, other_ref, up, down, act_ref, lat_mine_ref, lat_other_ref, cot):
        me = lax.axis_index("expert")
        all_experts = mine_ref.shape[0] - rows
        ids = lax.broadcasted_iota(jnp.int32, (all_experts, 128), 0)
        slots = lax.broadcasted_iota(jnp.int32, (all_experts, 128), 1)
        pick = jnp.where(ids == slots + me * local_experts, 1.0, 0.0).astype(BF16)
        probs = []
        for src, place in ((mine_ref, 0), (other_ref, half)):
            cot[pl.ds(place, half), :] = src[half:rows, :]
            probs.append(mxu(src[rows:, :half], pick, TN))
        probs = jnp.concatenate(probs, axis=0)
        total = None
        for i in range(local_experts):
            columns = pl.ds(i * hidden, hidden)
            other = jnp.maximum(mxu(other_ref[:half, :], up[i]), 0.0)
            positive = jnp.concatenate([positive_ref[:, columns], other], axis=0)
            weighted = positive * probs[:, i : i + 1]
            act_ref[:, columns] = (positive * weighted).astype(BF16)
            grad_act = mxu(cot[...], down[i], NT)
            grad_pre = (grad_act * (2.0 * weighted)).astype(BF16)
            term = mxu(grad_pre, up[i], NT)
            total = term if total is None else total + term
        lat_mine_ref[...] = total[:half].astype(BF16)
        lat_other_ref[...] = total[half:].astype(BF16)

    return local(
        body,
        (shape(rows, local_experts * hidden), shape(half, width), shape(half, width)),
        (positive, mine, other, up_weight, down_weight),
        "experts",
        scratch=[pltpu.VMEM((rows, width), BF16)],
        limit=24,
        flops=2 * 5 * half * width * hidden * local_experts,
    )


def outputs(act, down_weight, half):
    local_experts, hidden, width = down_weight.shape

    def body(act_ref, down, mine_ref, other_ref):
        total = None
        for i in range(local_experts):
            term = mxu(act_ref[:, pl.ds(i * hidden, hidden)], down[i])
            total = term if total is None else total + term
        mine_ref[...] = total[:half].astype(BF16)
        other_ref[...] = total[half:].astype(BF16)

    return local(
        body,
        (shape(half, width), shape(half, width)),
        (act, down_weight),
        "outputs",
        limit=16,
        flops=4 * half * local_experts * hidden * width,
    )


def pieces_of(first, second, chips, ties=()):
    rows, width = first.shape
    tok = rows // chips

    def body(first_ref, second_ref, *out_refs):
        chip = lax.axis_index("expert") // 2
        for mask in range(chips):
            rows = block(chip ^ mask, tok)
            out_refs[mask][...] = add_bf16(first_ref[rows, :], second_ref[rows, :])

    return local(body, tuple(shape(tok, width) for _ in range(chips)), (first, second), "pieces", ties=ties)


def scatter(pieces):
    return [xor_permute(pieces[k], "expert", 2 * k) for k in range(1, len(pieces))]


def add_pieces(pieces, start=0, ties=()):
    rows, width = pieces[0].shape

    def body(*refs):
        total = refs[0][...].astype(F32)
        for ref in refs[1:-1]:
            total = total + ref[pl.ds(start, rows), :].astype(F32)
        refs[-1][...] = total.astype(BF16)

    return local(body, shape(rows, width), tuple(pieces), "add_pieces", ties=ties)


def stack(values, rows, ties=(), flops=0):
    width = values[0].shape[1]

    def body(*refs):
        for i, ref in enumerate(refs[:-1]):
            refs[-1][pl.ds(i * rows, rows), :] = ref[pl.ds(0, rows), :]

    return local(body, shape(len(values) * rows, width), tuple(values), "stack", ties=ties, flops=flops)


def arrange(value, chips, tok, tie):
    count, rows, features = value.shape

    def body(x_ref, out_ref):
        me = lax.axis_index("expert")
        group = lax.axis_index("dp") if count > 1 else 0
        for side in range(2 * chips):
            for mask in range(count):
                out_ref[pl.ds((side * count + mask) * tok, tok), :] = x_ref[
                    group ^ mask, block(me ^ side, tok), :
                ]

    return local(body, shape(count * rows, features), (value,), "arrange", ties=(tie,))


def finish(x_rows, near, twins, far, in_proj, tok):
    rows, features = x_rows.shape
    width = near.shape[1]
    sides = 2 * near.shape[0] // tok
    count = rows // tok // sides
    far = [piece for pair in far for piece in pair]
    given = (x_rows, near, twins, in_proj, *far)
    steps = STEPS if features % (128 * STEPS) == 0 else 1
    tile = features // steps

    def body(*refs):
        x_ref, near_ref, twins_ref, in_proj_ref = refs[:4]
        far_refs = refs[4 : len(given)]
        input_ref, proj_ref, rows_ref, whole_ref, own_ref, result_ref, sems = refs[len(given) :]
        me = lax.axis_index("expert")
        for side in range(sides):
            src = (near_ref, twins_ref)[side % 2]
            piece = src[pl.ds(side // 2 * tok, tok), :]
            rows_ref[pl.ds(side * count * tok, tok), :] = piece
            own_ref[block(me ^ side, tok), :] = piece
            if far_refs:
                rows_ref[pl.ds((side * count + 1) * tok, (count - 1) * tok), :] = far_refs[side][...]
        copies = []
        for i in range(steps):
            part = pl.ds(i * tile, tile)
            whole_ref[part, :] = mxu(x_ref[:, part], rows_ref[...], TN)
            copies.append(pltpu.make_async_copy(whole_ref.at[part], proj_ref.at[part], sems.at[i]))
            copies[-1].start()
        result_ref[...] = mxu(own_ref[...], in_proj_ref[...], NT).astype(BF16)
        copies.append(pltpu.make_async_copy(result_ref, input_ref, sems.at[steps]))
        copies[-1].start()
        for copy in copies:
            copy.wait()

    own_rows = sides * tok
    return pl.pallas_call(
        body,
        out_shape=(shape(own_rows, features), shape(features, width, F32)),
        in_specs=[VMEM] * len(given),
        out_specs=(ANY, ANY),
        scratch_shapes=[
            pltpu.VMEM((rows, width), BF16),
            pltpu.VMEM((features, width), F32),
            pltpu.VMEM((own_rows, width), BF16),
            pltpu.VMEM((own_rows, features), BF16),
            pltpu.SemaphoreType.DMA((steps + 1,)),
        ],
        compiler_params=pltpu.CompilerParams(vmem_limit_bytes=24 * MIB),
        cost_estimate=pl.CostEstimate(
            flops=2 * rows * features * width, bytes_accessed=4 * MIB, transcendentals=0
        ),
        name="finish",
    )(*given)


def per_device(tokens_x, in_proj, up_weight, down_weight, expert_ids, route_probs, out_grad):
    owners = lax.axis_size("expert")
    groups = lax.axis_size("dp")
    chips = owners // 2
    chip = lax.axis_index("expert") // 2
    tok, top = expert_ids.shape
    all_experts = up_weight.shape[0] * owners
    features, width = in_proj.shape
    half = chips * tok
    bits = [1 << b for b in range(1, owners.bit_length() - 1)]
    gather_groups = groups == 4 and groups * owners * tok * width <= 1 << 22

    part_other, *sent, x_own = project(
        tokens_x, in_proj, out_grad, expert_ids, route_probs, all_experts
    )
    sums = (half // 2 + all_experts, half // 2)
    x_groups, x_spread = x_own[None], ()
    if gather_groups:
        x_spread = spread(x_own, groups)
        x_groups = lax.all_to_all(x_spread, "dp", split_axis=0, concat_axis=0, tiled=True)
    up, down = load(up_weight, down_weight)
    sent = streams(sent, xor_permute(part_other, "expert", 1), (x_spread,) if gather_groups else ())
    for step, stream_bits in enumerate(zip(bits, bits[::-1])):
        got = [xor_permute(value, "expert", bit) for value, bit in zip(sent, stream_bits)]
        if step + 1 < len(bits):
            sent = merge(sent, got, sums)
    mine = settle(sent, got, (order_of(bits), order_of(bits[::-1])), tok, all_experts, ties=(up, down))
    other = xor_permute(mine, "expert", 1)

    positive = preacts(mine, up, half)
    act, lat_mine, lat_other = experts(positive, mine, other, up, down)
    out_mine, out_other = outputs(act, down, half)
    out_pieces = pieces_of(out_mine, xor_permute(out_other, "expert", 1), chips)
    lat_pieces = pieces_of(lat_mine, xor_permute(lat_other, "expert", 1), chips)
    got = scatter(lat_pieces)
    latent_grad = add_pieces((lat_pieces[0], *got))

    own = ()
    out_got = scatter(out_pieces)
    if gather_groups:
        across = [xor_permute(latent_grad, "dp", m) for m in range(1, groups)]
        own = stack(across, tok, ties=(x_groups, *out_got))
    after = (own,) if gather_groups else ()
    got = scatter([latent_grad] * chips)
    combined = add_pieces((out_pieces[0], *out_got))
    near = stack([latent_grad, *got], tok, ties=after)
    parts = 2
    split = near.shape[0] // parts
    twins = [xor_permute(near[i * split : (i + 1) * split], "expert", 1) for i in range(parts)]
    twins = jnp.concatenate(twins, axis=0)
    x_rows = arrange(x_groups, chips, tok, latent_grad)
    far = []
    if gather_groups:
        pieces = [own] + [xor_permute(own, "expert", 2 * k) for k in range(1, chips)]
        far = [(piece, xor_permute(piece, "expert", 1)) for piece in pieces]
    input_grad, proj_grad = finish(x_rows, near, twins, far, in_proj, tok)
    if not gather_groups:
        proj_grad = lax.psum(proj_grad, "dp")
    return (combined, input_grad, proj_grad)


def solution(mesh):
    return jax.shard_map(
        per_device,
        mesh=mesh,
        in_specs=(
            P("dp", "expert"),
            P("expert", None),
            P("expert", None, None),
            P("expert", None, None),
            P(("dp", "expert"), None),
            P(("dp", "expert"), None),
            P(("dp", "expert"), None),
        ),
        out_specs=(P(("dp", "expert"), None), P("dp", "expert"), P("expert", None)),
        check_vma=False,
    )
```
